32 devices in a mesh: seq: 8 (over z, y), ch: 4 (over x, core).
Axes of the slice: x: 2, y: 2, z: 4, core: 2. Of those that a mesh axis runs over, the one named last changes fastest.
Arguments:
- query_proj: bfloat16 [1024, 2048], P('seq', 'ch'), may hold values from -6 to 6
- key_proj: bfloat16 [1024, 2048], P('seq', 'ch'), may hold values from -6 to 6
- value_proj: bfloat16 [1024, 2048], P('seq', 'ch'), may hold values from -6 to 6
- short_filter: float32 [3, 3, 2048], P(None, None, 'ch'), may hold values from -3.5 to 3.5
- long_filter: float32 [1024, 2048], P('seq', 'ch'), may hold values from -0.1875 to 0.1875
- skip_gain: float32 [2048], P('ch'), may hold values from 0.5 to 1.5
- out_weight: bfloat16 [2048, 4096], P('ch'), may hold values from -0.125 to 0.125
- cotangent: bfloat16 [1024, 4096], P('seq', 'ch'), may hold values from -6 to 6
Outputs:
- layer_out: bfloat16 [1024, 4096], P('seq', 'ch')
- grad_query: float32 [1024, 2048], P('seq', 'ch')
- grad_key: float32 [1024, 2048], P('seq', 'ch')
- grad_value: float32 [1024, 2048], P('seq', 'ch')
- grad_short: float32 [3, 3, 2048], P(None, None, 'ch')
- grad_filter: float32 [1024, 2048], P('seq', 'ch')
- grad_skip: float32 [2048], P('ch')
- grad_w_out_t: float32 [4096, 2048], P('seq', 'ch')
The draws below stay inside these ranges and needn't reach their ends.
All inputs are finite; a program needn't handle non-finite values.
Results may differ from the reference program's by a relative error of at most 0.011.
Values may be sent and summed in bfloat16 or wider, within the bound.
No kernel may reach another device: no remote copies, remote signals or barrier semaphores. Data moves between devices by JAX's collectives and lax.ppermute only.
A program may use at most 128 MiB of HBM per device.

```python
import jax
import jax.numpy as jnp

D = 4096
C = 2048
KS = 3
L = 1024


def spiked(values, own_key, source, target, shards_of, factor):
    def block_of(dim):
        return (jnp.arange(values.shape[dim]) // (values.shape[dim] // shards_of)).reshape((-1,) + (1,) * (values.ndim - 1 - dim))

    one_side = jax.random.permutation(own_key, shards_of)[block_of(target)]
    far = (block_of(target) + shards_of // 2) % shards_of
    return jnp.where((block_of(source) == one_side) | (block_of(source) == far), factor * values, values)


def shard_levels(rng, shape, pieces, smallest, high):
    level, own = 1.0, jax.random.fold_in(rng, 6)
    for axis_at, shards_of in pieces:
        steps = jnp.exp(jax.random.uniform(jax.random.fold_in(own, axis_at), (shards_of,), jnp.float32, smallest / len(pieces), high / len(pieces)))
        level = level * jnp.repeat(steps, shape[axis_at] // shards_of).reshape([-1 if axis == axis_at else 1 for axis in range(len(shape))])
    return level


def normal_values(own_key, dims, width, limit, shards=(), held_as=jnp.bfloat16):
    entries = jax.random.normal(own_key, dims, jnp.float32) * width
    if len(shards) > 0:
        entries = shard_levels(own_key, dims, shards, -0.22, 0.18) * entries
    return jnp.clip(entries, min=-limit, max=limit).astype(held_as)


def gaussian_with(rng, extent, scale, limit, cuts, heavy, kind=jnp.bfloat16):
    result = scale * jax.random.normal(rng, extent, jnp.float32)
    if cuts:
        result = result * shard_levels(rng, extent, cuts, -0.22, 0.18)
    return jnp.clip(spiked(result, jax.random.fold_in(rng, 3), *heavy), -limit, limit).astype(kind)


def setup_inputs(seed: int = 0) -> dict:
    key_list = jax.random.split(jax.random.key(seed), 9)
    return {
        "query_proj": normal_values(key_list[0], (L, C), 1.0, 6.0, ((0, 8), (1, 4))),
        "key_proj": normal_values(key_list[1], (L, C), 1.0, 6.0, ((0, 8), (1, 4))),
        "value_proj": normal_values(key_list[2], (L, C), 1.0, 6.0, ((0, 8), (1, 4))),
        "short_filter": normal_values(key_list[3], (3, KS, C), KS ** -0.5, 3.5, ((2, 4),), jnp.float32),
        "long_filter": normal_values(key_list[4], (L, C), L ** -0.5, 0.1875, ((0, 8), (1, 4)), jnp.float32),
        "skip_gain": jnp.clip(0.5 + 1.0 * jax.random.uniform(key_list[5], (C,), jnp.float32) ** shard_levels(key_list[5], (C,), ((0, 4),), -0.2, 0.2), 0.5, 1.5),
        "out_weight": normal_values(key_list[6], (C, D), C ** -0.5, 0.125, ((0, 4),)),
        "cotangent": gaussian_with(key_list[7], (L, D), 1.0, 6.0, ((0, 8), (1, 4)), (0, 1, 8, 2.0)),
    }


def causal_conv(signal, kernel):
    length = signal.shape[0]
    spectrum = jnp.fft.rfft(signal, n=2 * length, axis=0) * jnp.fft.rfft(kernel, n=2 * length, axis=0)
    return jnp.fft.irfft(spectrum, n=2 * length, axis=0)[:length].astype(signal.dtype)


def correlate(signal, kernel):
    length = signal.shape[0]
    spectrum = jnp.conj(jnp.fft.rfft(kernel, n=2 * length, axis=0)) * jnp.fft.rfft(signal, n=2 * length, axis=0)
    return jnp.fft.irfft(spectrum, n=2 * length, axis=0)[:length].astype(signal.dtype)


def reference(query_proj, key_proj, value_proj, short_filter, long_filter, skip_gain, out_weight, cotangent):
    streams = jnp.stack([query_proj, key_proj, value_proj]).astype(jnp.float32)
    row_count = streams.shape[1]
    padded = jnp.pad(streams, ((0, 0), (KS - 1, 0), (0, 0)))
    shifted = [padded[:, KS - 1 - offset:KS - 1 - offset + row_count] for offset in range(KS)]
    filtered = sum(short_filter[:, offset][:, None, :] * shifted[offset] for offset in range(KS))
    query_short, key_short, value_short = filtered[0], filtered[1], filtered[2]
    product = key_short * value_short
    mixed_seq = causal_conv(product, long_filter) + skip_gain * product
    gated_values = (query_short * mixed_seq).astype(jnp.bfloat16)
    layer_out = jnp.dot(gated_values, out_weight, preferred_element_type=jnp.float32).astype(jnp.bfloat16)
    grad_gated = jnp.dot(cotangent, out_weight.T, preferred_element_type=jnp.float32)
    grad_w_out_t = jnp.dot(cotangent.T, gated_values, preferred_element_type=jnp.float32)
    grad_mixed = grad_gated * query_short
    grad_query_short = grad_gated * mixed_seq
    grad_product = correlate(grad_mixed, long_filter) + skip_gain * grad_mixed
    grad_filter = correlate(grad_mixed, product)
    grad_skip = jnp.sum(grad_mixed * product, axis=0)
    grad_streams = jnp.stack([grad_query_short, grad_product * value_short, grad_product * key_short])
    grad_short = jnp.stack([jnp.sum(grad_streams * shifted[offset], axis=1) for offset in range(KS)], axis=1)
    tail_pad = jnp.pad(grad_streams, ((0, 0), (0, KS - 1), (0, 0)))
    grad_inputs = sum(short_filter[:, offset][:, None, :] * tail_pad[:, offset:offset + row_count] for offset in range(KS))
    return (layer_out, grad_inputs[0], grad_inputs[1], grad_inputs[2], grad_short, grad_filter, grad_skip, grad_w_out_t)
```

```python
import functools
import math

import jax
import jax.numpy as jnp
import ml_dtypes
import numpy as np
from jax import lax
from jax.experimental import pallas as pl
from jax.experimental.pallas import tpu as pltpu
from jax.sharding import PartitionSpec as P

exact_mode = lax.Precision.HIGHEST


def from_behind(shard, axis, by):
    size = lax.axis_size(axis)
    pairs = [(i, i + by) for i in range(size) if 0 <= i + by < size]
    return lax.ppermute(shard, axis, pairs)


def as_sent(shard):

    def short(part):
        return part.astype(jnp.bfloat16) if part.dtype == jnp.float32 else part

    return jax.tree.map(short, shard)


def tables(rows_out, cols_in, period):
    row_index = lax.broadcasted_iota(jnp.int32, (rows_out, cols_in), 0)
    col_index = lax.broadcasted_iota(jnp.int32, (rows_out, cols_in), 1)
    phase_angle = (row_index * col_index % period).astype(jnp.float32) * (2.0 * math.pi / period)
    return (jnp.cos(phase_angle), jnp.sin(phase_angle))


def along_rows(factor, values):
    return jnp.tensordot(factor, values, axes=1, precision=exact_mode)


def rows_spectrum(signal, basis_pair):
    return (along_rows(basis_pair[0], signal), -along_rows(basis_pair[1], signal))


def rows_inverse(complex_pair, basis_pair):
    total = along_rows(basis_pair[0], complex_pair[0]) - along_rows(basis_pair[1], complex_pair[1])
    return total / basis_pair[0].shape[1]


def block_forward(complex_pair, basis_pair):
    cosine_part, sine_part = basis_pair
    real_part = along_rows(cosine_part, complex_pair[0]) + along_rows(sine_part, complex_pair[1])
    imag_part = along_rows(cosine_part, complex_pair[1]) - along_rows(sine_part, complex_pair[0])
    return (real_part, imag_part)


def block_inverse(complex_pair, basis_pair):
    cosine_part, sine_part = basis_pair
    norming = 1.0 / cosine_part.shape[1]
    real_part = along_rows(cosine_part, complex_pair[0]) - along_rows(sine_part, complex_pair[1])
    imag_part = along_rows(cosine_part, complex_pair[1]) + along_rows(sine_part, complex_pair[0])
    return (real_part * norming, imag_part * norming)


def complex_product(first_pair, second_pair):
    return (
        first_pair[0] * second_pair[0] - first_pair[1] * second_pair[1],
        first_pair[0] * second_pair[1] + first_pair[1] * second_pair[0],
    )


def conj_product(first_pair, second_pair):
    return (
        first_pair[0] * second_pair[0] + first_pair[1] * second_pair[1],
        first_pair[0] * second_pair[1] - first_pair[1] * second_pair[0],
    )


def on_device(
    query_proj, key_proj, value_proj, short_filter, long_filter, skip_gain, out_weight, cotangent
):
    block_rows = query_proj.shape[0]
    tap_count = short_filter.shape[1]
    block_count = lax.axis_size("seq")
    streams = jnp.stack([query_proj, key_proj, value_proj])
    earlier = from_behind(streams[:, block_rows - (tap_count - 1) :], "seq", 1)
    extended = jnp.concatenate([earlier, streams], axis=1).astype(jnp.float32)
    shifted = [
        extended[:, tap_count - 1 - offset : tap_count - 1 - offset + block_rows]
        for offset in range(tap_count)
    ]
    filtered = sum(
        (short_filter[:, offset][:, None, :] * shifted[offset] for offset in range(tap_count))
    )
    query_short, key_short, value_short = (filtered[0], filtered[1], filtered[2])
    product = key_short * value_short
    forward_basis = tables(2 * block_rows, block_rows, 2 * block_rows)
    full_basis = tables(2 * block_rows, 2 * block_rows, 2 * block_rows)
    half_basis = tables(block_rows, 2 * block_rows, 2 * block_rows)
    block_basis = tables(2 * block_count, block_count, 2 * block_count)
    return_basis = tables(block_count, 2 * block_count, 2 * block_count)
    input_pair = rows_spectrum(product, forward_basis)
    filter_pair = rows_spectrum(long_filter, forward_basis)
    moved_data = (
        lax.all_to_all(input_pair[0][None], "seq", split_axis=1, concat_axis=0, tiled=True),
        lax.all_to_all(input_pair[1][None], "seq", split_axis=1, concat_axis=0, tiled=True),
        lax.all_to_all(filter_pair[0][None], "seq", split_axis=1, concat_axis=0, tiled=True),
        lax.all_to_all(filter_pair[1][None], "seq", split_axis=1, concat_axis=0, tiled=True),
    )
    input_spectrum = block_forward((moved_data[0], moved_data[1]), block_basis)
    filter_spectrum = block_forward((moved_data[2], moved_data[3]), block_basis)
    inverse_pair = block_inverse(complex_product(filter_spectrum, input_spectrum), return_basis)
    returned = (
        lax.all_to_all(inverse_pair[0], "seq", split_axis=0, concat_axis=1, tiled=True),
        lax.all_to_all(inverse_pair[1], "seq", split_axis=0, concat_axis=1, tiled=True),
    )
    folded = rows_inverse((returned[0][0], returned[1][0]), full_basis)
    carried = from_behind(folded[block_rows:], "seq", 1)
    convolved = folded[:block_rows] + carried
    mixed_seq = convolved + skip_gain * product
    gated_values = (query_short * mixed_seq).astype(jnp.bfloat16)
    partial_value = jnp.dot(gated_values, out_weight, preferred_element_type=jnp.float32)
    layer_out = lax.psum_scatter(partial_value, "ch", scatter_dimension=1, tiled=True).astype(
        jnp.bfloat16
    )
    full_cotangent = lax.all_gather(cotangent, "ch", axis=1, tiled=True)
    grad_gated = lax.dot_general(
        full_cotangent, out_weight, (((1,), (1,)), ((), ())), preferred_element_type=jnp.float32
    )
    grad_w_out_t = lax.psum_scatter(
        lax.dot_general(
            full_cotangent,
            gated_values,
            (((0,), (0,)), ((), ())),
            preferred_element_type=jnp.float32,
        ),
        "seq",
        scatter_dimension=0,
        tiled=True,
    )
    grad_mixed = grad_gated * query_short
    grad_query_short = grad_gated * mixed_seq
    following = from_behind(grad_mixed.astype(jnp.bfloat16), "seq", -1).astype(grad_mixed.dtype)
    spread = jnp.concatenate([grad_mixed, following], axis=0)
    grad_pair = rows_spectrum(spread, full_basis)
    moved_grad = (
        lax.all_to_all(
            grad_pair[0][None].astype(jnp.bfloat16), "seq", split_axis=1, concat_axis=0, tiled=True
        ).astype(jnp.float32),
        lax.all_to_all(
            grad_pair[1][None].astype(jnp.bfloat16), "seq", split_axis=1, concat_axis=0, tiled=True
        ).astype(jnp.float32),
    )
    grad_spectrum = block_forward(moved_grad, block_basis)
    input_back = block_inverse(conj_product(filter_spectrum, grad_spectrum), return_basis)
    filter_back = block_inverse(conj_product(input_spectrum, grad_spectrum), return_basis)
    returned_grad = (
        lax.all_to_all(as_sent(input_back[0]), "seq", split_axis=0, concat_axis=1, tiled=True),
        lax.all_to_all(as_sent(input_back[1]), "seq", split_axis=0, concat_axis=1, tiled=True),
        lax.all_to_all(as_sent(filter_back[0]), "seq", split_axis=0, concat_axis=1, tiled=True),
        lax.all_to_all(as_sent(filter_back[1]), "seq", split_axis=0, concat_axis=1, tiled=True),
    )
    conv_grad = rows_inverse((returned_grad[0][0], returned_grad[1][0]), half_basis)
    grad_filter = rows_inverse((returned_grad[2][0], returned_grad[3][0]), half_basis)
    grad_product = conv_grad + skip_gain * grad_mixed
    grad_streams = jnp.stack(
        [grad_query_short, grad_product * value_short, grad_product * key_short]
    )
    later_rows = from_behind(grad_streams[:, : tap_count - 1], "seq", -1)
    padded_grad = jnp.concatenate([grad_streams, later_rows], axis=1)
    grad_inputs = sum(
        (
            short_filter[:, offset][:, None, :] * padded_grad[:, offset : offset + block_rows]
            for offset in range(tap_count)
        )
    )
    short_terms = jnp.stack(
        [jnp.sum(grad_streams * shifted[offset], axis=1) for offset in range(tap_count)], axis=1
    )
    skip_terms = jnp.sum(grad_mixed * product, axis=0)
    grad_short, grad_skip = lax.psum((short_terms, skip_terms), "seq")
    return (
        layer_out,
        grad_inputs[0],
        grad_inputs[1],
        grad_inputs[2],
        grad_short,
        grad_filter,
        grad_skip,
        grad_w_out_t,
    )


LANES = 128
HALF = 64
F32 = jnp.float32
BF16 = jnp.bfloat16


def swap_bits(shard, axis, mask):
    size = lax.axis_size(axis)
    return lax.ppermute(shard, axis, [(i, i ^ mask) for i in range(size)])


@functools.lru_cache
def wave_tables(rows):
    steps = np.outer(2 * np.arange(rows) + 1, np.arange(rows)) % (4 * rows)
    angle = steps * (math.pi / (2 * rows))
    cosine, sine = np.cos(angle), np.sin(angle)
    inverse = np.concatenate([cosine.T, sine.T], axis=1) / rows
    forward = np.concatenate([cosine, sine], axis=0)
    return forward.astype(ml_dtypes.bfloat16), inverse.astype(ml_dtypes.bfloat16)


def left_lanes(rows):
    return lax.broadcasted_iota(jnp.int32, (rows, LANES), 1) < HALF


def other_half(block):
    return pltpu.roll(block, HALF, 1)


def earlier_rows(block, by):
    if by == 0:
        return block
    row = lax.broadcasted_iota(jnp.int32, block.shape, 0)
    return jnp.where(row >= by, pltpu.roll(block, by, 0), 0.0)


def later_rows(block, by):
    if by == 0:
        return block
    size = block.shape[0]
    row = lax.broadcasted_iota(jnp.int32, block.shape, 0)
    return jnp.where(row < size - by, pltpu.roll(block, size - by, 0), 0.0)


def big_dot(matrix_ref, operand, out_ref, step=256):
    for start in range(0, matrix_ref.shape[0], step):
        out_ref[start : start + step] = jnp.dot(
            matrix_ref[start : start + step], operand, preferred_element_type=F32
        )


def pack_streams_kernel(q_ref, k_ref, v_ref, h_ref, out_ref):
    rows = q_ref.shape[0]
    left = left_lanes(rows)
    for peer in range(out_ref.shape[0]):
        lanes = slice(LANES * (peer // 2), LANES * (peer // 2) + LANES)
        pairs = ((k_ref, q_ref), (v_ref, h_ref))
        for at, (first_ref, second_ref) in enumerate(pairs):
            first = first_ref[:, lanes].astype(F32)
            second = second_ref[:, lanes].astype(F32)
            if peer % 2 == 0:
                both = jnp.where(left, first, other_half(second))
            else:
                both = jnp.where(left, other_half(first), second)
            out_ref[peer, at] = both.astype(BF16)


def grad_gated_kernel(ids_ref, c0_ref, c1_ref, c2_ref, c3_ref, w_ref, out_ref):
    mine = ids_ref[1]
    width = c0_ref.shape[1]
    total = None
    for mask, part_ref in enumerate((c0_ref, c1_ref, c2_ref, c3_ref)):
        at = pl.multiple_of((mine ^ mask) * width, width)
        term = lax.dot_general(
            part_ref[...],
            w_ref[:, pl.ds(at, width)],
            (((1,), (1,)), ((), ())),
            preferred_element_type=F32,
        )
        total = term if total is None else total + term
    out_ref[...] = total.astype(BF16)


def forward_kernel(
    ids_ref, moved_ref, prm_ref, fwd_ref, inv_ref, gg_ref, c0_ref, c1_ref, c2_ref, c3_ref,
    send_ref, kqs_ref, vhs_ref, mq_ref, spec_ref, y_ref,
):
    peers, _, rows, _ = moved_ref.shape
    size = peers * rows
    left = left_lanes(size)
    kq = moved_ref[:, 0].reshape(size, LANES).astype(F32)
    vh = moved_ref[:, 1].reshape(size, LANES).astype(F32)
    kqs = sum(prm_ref[j : j + 1] * earlier_rows(kq, j) for j in range(3))
    vhs = sum(prm_ref[3 + j : 4 + j] * earlier_rows(vh, j) for j in range(3))
    kqs_ref[...] = kqs
    vhs_ref[...] = vhs
    product = kqs * vhs
    big_dot(fwd_ref, jnp.where(left, product, vhs).astype(BF16), spec_ref)
    xc, xs = spec_ref[:size], spec_ref[size:]
    hc, hs = other_half(xc), other_half(xs)
    y_parts = jnp.concatenate([xc * hc - xs * hs, xc * hs + xs * hc], axis=0).astype(BF16)
    big_dot(inv_ref, y_parts, y_ref)
    both_product = jnp.where(left, product, other_half(product))
    mixed = y_ref[...] + prm_ref[12:13] * both_product
    mq_ref[...] = jnp.where(left, mixed, kqs)
    gated = kqs * mixed
    left_rows = left_lanes(rows)
    for peer in range(peers):
        lanes = slice(LANES * (peer // 2), LANES * (peer // 2) + LANES)
        gg = gg_ref[:, lanes].astype(F32)
        if peer % 2 == 1:
            gg = other_half(gg)
        mine = gated[rows * peer : rows * peer + rows]
        send_ref[peer, :rows] = jnp.where(left_rows, gg, mine).astype(BF16)
    own = ids_ref[1]
    for mask, part_ref in enumerate((c0_ref, c1_ref, c2_ref, c3_ref)):
        for half in range(2):
            at = pl.multiple_of(half * 4 * LANES + own * LANES, LANES)
            send_ref[2 * (own ^ mask) + half, rows:] = part_ref[:, pl.ds(at, LANES)]


def project_kernel(ids_ref, moved_ref, w_ref, gated_ref, keep_ref, send_ref, cot_ref):
    peers = moved_ref.shape[0]
    rows = moved_ref.shape[1] // 2
    left = left_lanes(rows)
    for tile in range(peers // 2):
        first = moved_ref[2 * tile, :rows].astype(F32)
        second = moved_ref[2 * tile + 1, :rows].astype(F32)
        both = jnp.where(left, other_half(first), second)
        gated_ref[:, LANES * tile : LANES * tile + LANES] = both.astype(BF16)
    cot_ref[...] = moved_ref[:, rows:]
    gated = gated_ref[...]
    mine = ids_ref[1]
    width = keep_ref.shape[2]
    for mask in (1, 3, 0, 2):
        at = pl.multiple_of((mine ^ mask) * width, width)
        part = jnp.dot(gated, w_ref[:, pl.ds(at, width)], preferred_element_type=F32)
        if mask % 2 == 1:
            send_ref[mask // 2] = part.astype(BF16)
        else:
            keep_ref[mask // 2] = part


def backward_kernel(
    streams_ref, moved_ref, prm_ref, fwd_ref, inv_ref, kqs_ref, vhs_ref, mq_ref, spec_ref,
    send_ref, mspec_ref, back_ref,
):
    peers, _, rows, _ = streams_ref.shape
    size = peers * rows
    left = left_lanes(size)
    gg = moved_ref[:, :rows].reshape(size, LANES).astype(F32)
    gg = jnp.where(left, gg, other_half(gg))
    z = gg * mq_ref[...]
    grad_mixed = jnp.where(left, other_half(z), z)
    big_dot(fwd_ref, grad_mixed.astype(BF16), mspec_ref)
    xc, xs = spec_ref[:size], spec_ref[size:]
    mc, ms = mspec_ref[:size], mspec_ref[size:]
    parts = jnp.concatenate([xc * mc + xs * ms, xc * ms - xs * mc], axis=0).astype(BF16)
    big_dot(inv_ref, parts, back_ref)
    back = back_ref[...]
    kqs, vhs = kqs_ref[...], vhs_ref[...]
    grad_product = back + prm_ref[12:13] * grad_mixed
    grad_product = jnp.where(left, other_half(grad_product), grad_product)
    grad_kv = grad_product * jnp.where(left, vhs, other_half(kqs))
    grad_qf = jnp.where(left, z, back)
    grad_qf = jnp.where(left, z, other_half(back))
    kq = streams_ref[:, 0].reshape(size, LANES).astype(F32)
    vh = streams_ref[:, 1].reshape(size, LANES).astype(F32)
    raw_kv = jnp.where(left, kq, other_half(vh))
    raw_q = other_half(kq)
    out_kv = sum(prm_ref[6 + j : 7 + j] * later_rows(grad_kv, j) for j in range(3))
    out_qf = sum(prm_ref[9 + j : 10 + j] * later_rows(grad_qf, j) for j in range(3))
    sums = [jnp.sum(grad_kv * earlier_rows(raw_kv, j), axis=0, keepdims=True) for j in range(3)]
    sums += [jnp.sum(grad_qf * earlier_rows(raw_q, j), axis=0, keepdims=True) for j in range(3)]
    sums += [jnp.sum(grad_mixed * kqs * vhs, axis=0, keepdims=True)]
    sums += [jnp.zeros_like(sums[0])]
    small = jnp.concatenate(sums, axis=0)
    small_high = small.astype(BF16).astype(F32)
    small = jnp.concatenate([small_high, small - small_high], axis=0).astype(BF16)
    for peer in range(peers):
        at = slice(rows * peer, rows * peer + rows)
        send_ref[peer, :rows] = out_kv[at].astype(BF16)
        send_ref[peer, rows : 2 * rows] = out_qf[at].astype(BF16)
        send_ref[peer, 2 * rows :] = small


def unpack_kernel(moved_ref, q_ref, k_ref, v_ref, f_ref, short_ref, skip_ref):
    peers = moved_ref.shape[0]
    rows = q_ref.shape[0]
    left = left_lanes(rows)
    left_few = left_lanes(8)

    def merged(first, second, mask):
        return (
            jnp.where(mask, first, other_half(second)),
            jnp.where(mask, other_half(first), second),
        )

    for tile in range(peers // 2):
        lanes = slice(LANES * tile, LANES * tile + LANES)
        first, second = moved_ref[2 * tile].astype(F32), moved_ref[2 * tile + 1].astype(F32)
        k_ref[:, lanes], v_ref[:, lanes] = merged(first[:rows], second[:rows], left)
        q_ref[:, lanes], f_ref[:, lanes] = merged(
            first[rows : 2 * rows], second[rows : 2 * rows], left
        )
        few = [part[2 * rows : 2 * rows + 8] + part[2 * rows + 8 :] for part in (first, second)]
        low, high = merged(few[0], few[1], left_few)
        short_ref[0, :, lanes] = low[3:6]
        short_ref[1, :, lanes] = low[0:3]
        short_ref[2, :, lanes] = high[0:3]
        skip_ref[:, lanes] = low[6:7]


def grad_weight_kernel(ids_ref, *refs):
    out_ref = refs[-1]
    cots, gates = refs[:4], refs[4:-1]
    own_row, own = ids_ref[0], ids_ref[1]
    for mask, cot_ref in enumerate(cots):
        total = None
        for at, gate_ref in enumerate(gates):
            term = lax.dot_general(
                cot_ref[own_row ^ at],
                gate_ref[...],
                (((0,), (0,)), ((), ())),
                preferred_element_type=F32,
            )
            total = term if total is None else total + term
        out_ref[pl.ds(pl.multiple_of((own ^ mask) * LANES, LANES), LANES)] = total


def call(kernel, outs, scalars, *arrays, scratch=(), limit=32, flops=0):
    vmem = pl.BlockSpec(memory_space=pltpu.VMEM)
    smem = pl.BlockSpec(memory_space=pltpu.SMEM)
    many = isinstance(outs, list)
    moved = sum(math.prod(a.shape) * a.dtype.itemsize for a in arrays)
    return pl.pallas_call(
        kernel,
        out_shape=outs,
        in_specs=[smem] * len(scalars) + [vmem] * len(arrays),
        out_specs=[vmem] * len(outs) if many else vmem,
        scratch_shapes=list(scratch),
        compiler_params=pltpu.CompilerParams(vmem_limit_bytes=limit * 2**20),
        cost_estimate=pl.CostEstimate(flops=flops, bytes_accessed=moved, transcendentals=0),
    )(*scalars, *arrays)


def shaped(shape, dtype):
    return jax.ShapeDtypeStruct(shape, dtype)


def gathered_pairs(block, axis):
    near = swap_bits(block, axis, 1)
    far = swap_bits(block, axis, 2)
    return [block, near, far, swap_bits(far, axis, 1)]


def gathered_all(block, axis):
    blocks = {0: block}
    mask = lax.axis_size(axis) // 2
    while mask:
        blocks |= {at | mask: swap_bits(held, axis, mask) for at, held in blocks.items()}
        mask //= 2
    return [blocks[at] for at in range(len(blocks))]


def on_device_packed(
    query_proj, key_proj, value_proj, short_filter, long_filter, skip_gain, out_weight, cotangent
):
    peers = lax.axis_size("seq")
    rows, channels = query_proj.shape
    features = cotangent.shape[1]
    size = peers * rows
    seq_at, ch_at = lax.axis_index("seq"), lax.axis_index("ch")
    ids = jnp.stack([seq_at, ch_at]).astype(jnp.int32)
    forward_table, inverse_table = (jnp.asarray(table) for table in wave_tables(size))
    cots = gathered_pairs(cotangent, "ch")

    own_short = lax.dynamic_slice_in_dim(short_filter, seq_at * HALF, HALF, 2)
    own_skip = lax.dynamic_slice_in_dim(skip_gain, seq_at * HALF, HALF, 0)[None]
    unit = (lax.broadcasted_iota(jnp.int32, (3, HALF), 0) == 0).astype(F32)
    wq, wk, wv = own_short[0], own_short[1], own_short[2]
    prm = jnp.concatenate(
        [
            jnp.concatenate([wk, wv, wk, wq, own_skip], axis=0),
            jnp.concatenate([wq, unit, wv, unit, own_skip], axis=0),
        ],
        axis=1,
    )

    packed = call(
        pack_streams_kernel,
        shaped((peers, 2, rows, LANES), BF16),
        [],
        query_proj,
        key_proj,
        value_proj,
        long_filter,
    )
    streams = lax.all_to_all(packed, "seq", 0, 0, tiled=True)
    grad_gated = call(
        grad_gated_kernel,
        shaped((rows, channels), BF16),
        [ids],
        *cots,
        out_weight,
        flops=2 * rows * channels * 4 * features,
    )
    wide = shaped((size, LANES), F32)
    send, kqs, vhs, mq, spec = call(
        forward_kernel,
        [shaped((peers, 2 * rows, LANES), BF16), wide, wide, wide, shaped((2 * size, LANES), F32)],
        [ids],
        streams,
        prm,
        forward_table,
        inverse_table,
        grad_gated,
        *cots,
        scratch=[pltpu.VMEM((size, LANES), F32)],
        flops=8 * size * size * LANES,
    )
    moved = lax.all_to_all(send, "seq", 0, 0, tiled=True)
    gated, keep, away, cot_rows = call(
        project_kernel,
        [
            shaped((rows, channels), BF16),
            shaped((2, rows, features), F32),
            shaped((2, rows, features), BF16),
            shaped((peers, rows, LANES), BF16),
        ],
        [ids],
        moved,
        out_weight,
        flops=2 * rows * channels * 4 * features,
    )
    near = swap_bits(away, "ch", 1)
    passed = (keep[1] + near[1].astype(F32)).astype(BF16)
    layer_out = (keep[0] + near[0].astype(F32) + swap_bits(passed, "ch", 2).astype(F32)).astype(
        BF16
    )
    cot_parts = gathered_pairs(cot_rows, "ch")
    gates = gathered_all(gated, "seq")
    back = call(
        backward_kernel,
        shaped((peers, 2 * rows + 16, LANES), BF16),
        [],
        streams,
        moved,
        prm,
        forward_table,
        inverse_table,
        kqs,
        vhs,
        mq,
        spec,
        scratch=[pltpu.VMEM((2 * size, LANES), F32), pltpu.VMEM((size, LANES), F32)],
        flops=8 * size * size * LANES,
    )
    returned = lax.all_to_all(back, "seq", 0, 0, tiled=True)
    plain = shaped((rows, channels), F32)
    grad_query, grad_key, grad_value, grad_filter, grad_short, grad_skip = call(
        unpack_kernel,
        [plain, plain, plain, plain, shaped((3, 3, channels), F32), shaped((1, channels), F32)],
        [],
        returned,
    )
    grad_w_out_t = call(
        grad_weight_kernel,
        shaped((4 * LANES, channels), F32),
        [ids],
        *cot_parts,
        *gates,
        flops=2 * size * channels * 4 * LANES,
    )
    return (
        layer_out,
        grad_query,
        grad_key,
        grad_value,
        grad_short,
        grad_filter,
        grad_skip[0],
        grad_w_out_t,
    )


def solution(mesh):
    in_specs = (
        P("seq", "ch"),
        P("seq", "ch"),
        P("seq", "ch"),
        P(None, None, "ch"),
        P("seq", "ch"),
        P("ch"),
        P("ch", None),
        P("seq", "ch"),
    )
    out_specs = (
        P("seq", "ch"),
        P("seq", "ch"),
        P("seq", "ch"),
        P("seq", "ch"),
        P(None, None, "ch"),
        P("seq", "ch"),
        P("ch"),
        P("seq", "ch"),
    )
    split = dict(mesh.shape)

    def whole(*arrays):
        rows = arrays[0].shape[0] // split["seq"]
        channels = arrays[0].shape[1] // split["ch"]
        features = arrays[7].shape[1]
        packs = (
            split["ch"] == 4
            and channels == HALF * split["seq"]
            and features == 4 * LANES * split["seq"]
            and arrays[0].shape[0] <= 1024
            and rows % 16 == 0
            and arrays[3].shape[1] == 3
        )
        body = on_device_packed if packs else on_device
        return jax.shard_map(
            body,
            mesh=mesh,
            in_specs=in_specs,
            out_specs=out_specs,
            check_vma=False,
        )(*arrays)

    return whole
```

```python
import functools
import math

import jax
import jax.numpy as jnp
import ml_dtypes
import numpy as np
from jax import lax
from jax.experimental import pallas as pl
from jax.experimental.pallas import tpu as pltpu
from jax.sharding import PartitionSpec as P

exact_mode = lax.Precision.HIGHEST


def from_behind(shard, axis, by):
    size = lax.axis_size(axis)
    pairs = [(i, i + by) for i in range(size) if 0 <= i + by < size]
    return lax.ppermute(shard, axis, pairs)


def as_sent(shard):

    def short(part):
        return part.astype(jnp.bfloat16) if part.dtype == jnp.float32 else part

    return jax.tree.map(short, shard)


def tables(rows_out, cols_in, period):
    row_index = lax.broadcasted_iota(jnp.int32, (rows_out, cols_in), 0)
    col_index = lax.broadcasted_iota(jnp.int32, (rows_out, cols_in), 1)
    phase_angle = (row_index * col_index % period).astype(jnp.float32) * (2.0 * math.pi / period)
    return (jnp.cos(phase_angle), jnp.sin(phase_angle))


def along_rows(factor, values):
    return jnp.tensordot(factor, values, axes=1, precision=exact_mode)


def rows_spectrum(signal, basis_pair):
    return (along_rows(basis_pair[0], signal), -along_rows(basis_pair[1], signal))


def rows_inverse(complex_pair, basis_pair):
    total = along_rows(basis_pair[0], complex_pair[0]) - along_rows(basis_pair[1], complex_pair[1])
    return total / basis_pair[0].shape[1]


def block_forward(complex_pair, basis_pair):
    cosine_part, sine_part = basis_pair
    real_part = along_rows(cosine_part, complex_pair[0]) + along_rows(sine_part, complex_pair[1])
    imag_part = along_rows(cosine_part, complex_pair[1]) - along_rows(sine_part, complex_pair[0])
    return (real_part, imag_part)


def block_inverse(complex_pair, basis_pair):
    cosine_part, sine_part = basis_pair
    norming = 1.0 / cosine_part.shape[1]
    real_part = along_rows(cosine_part, complex_pair[0]) - along_rows(sine_part, complex_pair[1])
    imag_part = along_rows(cosine_part, complex_pair[1]) + along_rows(sine_part, complex_pair[0])
    return (real_part * norming, imag_part * norming)


def complex_product(first_pair, second_pair):
    return (
        first_pair[0] * second_pair[0] - first_pair[1] * second_pair[1],
        first_pair[0] * second_pair[1] + first_pair[1] * second_pair[0],
    )


def conj_product(first_pair, second_pair):
    return (
        first_pair[0] * second_pair[0] + first_pair[1] * second_pair[1],
        first_pair[0] * second_pair[1] - first_pair[1] * second_pair[0],
    )


def on_device(
    query_proj, key_proj, value_proj, short_filter, long_filter, skip_gain, out_weight, cotangent
):
    block_rows = query_proj.shape[0]
    tap_count = short_filter.shape[1]
    block_count = lax.axis_size("seq")
    streams = jnp.stack([query_proj, key_proj, value_proj])
    earlier = from_behind(streams[:, block_rows - (tap_count - 1) :], "seq", 1)
    extended = jnp.concatenate([earlier, streams], axis=1).astype(jnp.float32)
    shifted = [
        extended[:, tap_count - 1 - offset : tap_count - 1 - offset + block_rows]
        for offset in range(tap_count)
    ]
    filtered = sum(
        (short_filter[:, offset][:, None, :] * shifted[offset] for offset in range(tap_count))
    )
    query_short, key_short, value_short = (filtered[0], filtered[1], filtered[2])
    product = key_short * value_short
    forward_basis = tables(2 * block_rows, block_rows, 2 * block_rows)
    full_basis = tables(2 * block_rows, 2 * block_rows, 2 * block_rows)
    half_basis = tables(block_rows, 2 * block_rows, 2 * block_rows)
    block_basis = tables(2 * block_count, block_count, 2 * block_count)
    return_basis = tables(block_count, 2 * block_count, 2 * block_count)
    input_pair = rows_spectrum(product, forward_basis)
    filter_pair = rows_spectrum(long_filter, forward_basis)
    moved_data = (
        lax.all_to_all(input_pair[0][None], "seq", split_axis=1, concat_axis=0, tiled=True),
        lax.all_to_all(input_pair[1][None], "seq", split_axis=1, concat_axis=0, tiled=True),
        lax.all_to_all(filter_pair[0][None], "seq", split_axis=1, concat_axis=0, tiled=True),
        lax.all_to_all(filter_pair[1][None], "seq", split_axis=1, concat_axis=0, tiled=True),
    )
    input_spectrum = block_forward((moved_data[0], moved_data[1]), block_basis)
    filter_spectrum = block_forward((moved_data[2], moved_data[3]), block_basis)
    inverse_pair = block_inverse(complex_product(filter_spectrum, input_spectrum), return_basis)
    returned = (
        lax.all_to_all(inverse_pair[0], "seq", split_axis=0, concat_axis=1, tiled=True),
        lax.all_to_all(inverse_pair[1], "seq", split_axis=0, concat_axis=1, tiled=True),
    )
    folded = rows_inverse((returned[0][0], returned[1][0]), full_basis)
    carried = from_behind(folded[block_rows:], "seq", 1)
    convolved = folded[:block_rows] + carried
    mixed_seq = convolved + skip_gain * product
    gated_values = (query_short * mixed_seq).astype(jnp.bfloat16)
    partial_value = jnp.dot(gated_values, out_weight, preferred_element_type=jnp.float32)
    layer_out = lax.psum_scatter(partial_value, "ch", scatter_dimension=1, tiled=True).astype(
        jnp.bfloat16
    )
    full_cotangent = lax.all_gather(cotangent, "ch", axis=1, tiled=True)
    grad_gated = lax.dot_general(
        full_cotangent, out_weight, (((1,), (1,)), ((), ())), preferred_element_type=jnp.float32
    )
    grad_w_out_t = lax.psum_scatter(
        lax.dot_general(
            full_cotangent,
            gated_values,
            (((0,), (0,)), ((), ())),
            preferred_element_type=jnp.float32,
        ),
        "seq",
        scatter_dimension=0,
        tiled=True,
    )
    grad_mixed = grad_gated * query_short
    grad_query_short = grad_gated * mixed_seq
    following = from_behind(grad_mixed.astype(jnp.bfloat16), "seq", -1).astype(grad_mixed.dtype)
    spread = jnp.concatenate([grad_mixed, following], axis=0)
    grad_pair = rows_spectrum(spread, full_basis)
    moved_grad = (
        lax.all_to_all(
            grad_pair[0][None].astype(jnp.bfloat16), "seq", split_axis=1, concat_axis=0, tiled=True
        ).astype(jnp.float32),
        lax.all_to_all(
            grad_pair[1][None].astype(jnp.bfloat16), "seq", split_axis=1, concat_axis=0, tiled=True
        ).astype(jnp.float32),
    )
    grad_spectrum = block_forward(moved_grad, block_basis)
    input_back = block_inverse(conj_product(filter_spectrum, grad_spectrum), return_basis)
    filter_back = block_inverse(conj_product(input_spectrum, grad_spectrum), return_basis)
    returned_grad = (
        lax.all_to_all(as_sent(input_back[0]), "seq", split_axis=0, concat_axis=1, tiled=True),
        lax.all_to_all(as_sent(input_back[1]), "seq", split_axis=0, concat_axis=1, tiled=True),
        lax.all_to_all(as_sent(filter_back[0]), "seq", split_axis=0, concat_axis=1, tiled=True),
        lax.all_to_all(as_sent(filter_back[1]), "seq", split_axis=0, concat_axis=1, tiled=True),
    )
    conv_grad = rows_inverse((returned_grad[0][0], returned_grad[1][0]), half_basis)
    grad_filter = rows_inverse((returned_grad[2][0], returned_grad[3][0]), half_basis)
    grad_product = conv_grad + skip_gain * grad_mixed
    grad_streams = jnp.stack(
        [grad_query_short, grad_product * value_short, grad_product * key_short]
    )
    later_rows = from_behind(grad_streams[:, : tap_count - 1], "seq", -1)
    padded_grad = jnp.concatenate([grad_streams, later_rows], axis=1)
    grad_inputs = sum(
        (
            short_filter[:, offset][:, None, :] * padded_grad[:, offset : offset + block_rows]
            for offset in range(tap_count)
        )
    )
    short_terms = jnp.stack(
        [jnp.sum(grad_streams * shifted[offset], axis=1) for offset in range(tap_count)], axis=1
    )
    skip_terms = jnp.sum(grad_mixed * product, axis=0)
    grad_short, grad_skip = lax.psum((short_terms, skip_terms), "seq")
    return (
        layer_out,
        grad_inputs[0],
        grad_inputs[1],
        grad_inputs[2],
        grad_short,
        grad_filter,
        grad_skip,
        grad_w_out_t,
    )


LANES = 128
HALF = 64
LIMIT = 64 * 2**20 - 2**17
F32 = jnp.float32
BF16 = jnp.bfloat16


def swap_bits(shard, axis, mask):
    size = lax.axis_size(axis)
    return lax.ppermute(shard, axis, [(i, i ^ mask) for i in range(size)])


@functools.lru_cache
def wave_tables(rows):
    half = rows // 2
    steps = np.outer(2 * np.arange(half) + 1, np.arange(rows)) % (4 * rows)
    angle = steps * (math.pi / (2 * rows))
    waves = np.concatenate([np.cos(angle), np.sin(angle)], axis=0)
    split = np.stack([waves[:, 0::2], waves[:, 1::2]])
    inverse = np.swapaxes(split, 1, 2) / rows
    return split.astype(ml_dtypes.bfloat16), inverse.astype(ml_dtypes.bfloat16)


def left_lanes(rows):
    return lax.broadcasted_iota(jnp.int32, (rows, LANES), 1) < HALF


def other_half(block):
    return pltpu.roll(block, HALF, 1)


def earlier_rows(block, by):
    if by == 0:
        return block
    row = lax.broadcasted_iota(jnp.int32, block.shape, 0)
    return jnp.where(row >= by, pltpu.roll(block, by, 0), 0.0)


def later_rows(block, by):
    if by == 0:
        return block
    size = block.shape[0]
    row = lax.broadcasted_iota(jnp.int32, block.shape, 0)
    return jnp.where(row < size - by, pltpu.roll(block, size - by, 0), 0.0)


def spectrum(table_ref, signal_ref, out_ref):
    half = table_ref.shape[2]
    quarter = 256
    even = signal_ref[pl.ds(0, half, stride=2)].astype(BF16)
    odd = signal_ref[pl.ds(1, half, stride=2)].astype(BF16)
    for start in range(0, 2 * half, quarter):
        at = slice(start, start + quarter)
        first = jnp.dot(table_ref[0, at], even, preferred_element_type=F32)
        second = jnp.dot(table_ref[1, at], odd, preferred_element_type=F32)
        kind, row = (0, start) if start < half else (2, start - half)
        out_ref[kind, row : row + quarter] = first + second
        mirrored = first - second if kind == 0 else second - first
        out_ref[kind + 1, row : row + quarter] = mirrored


def from_spectrum(table_ref, parts, out_ref):
    half = table_ref.shape[1]
    quarter = 256
    cosine, cosine_mirror, sine, sine_mirror = parts
    even = jnp.concatenate([cosine + cosine_mirror, sine - sine_mirror], axis=0).astype(BF16)
    odd = jnp.concatenate([cosine - cosine_mirror, sine + sine_mirror], axis=0).astype(BF16)
    for side, operand in enumerate((even, odd)):
        for start in range(0, half, quarter):
            out_ref[pl.ds(2 * start + side, quarter, stride=2)] = jnp.dot(
                table_ref[side, start : start + quarter], operand, preferred_element_type=F32
            )


def fetch(pairs, sems):
    copies = [
        pltpu.make_async_copy(source, target, sems.at[at])
        for at, (source, target) in enumerate(pairs)
    ]
    for copy in copies:
        copy.start()
    return copies


def finish(copies):
    for copy in copies:
        copy.wait()


def pack_streams_kernel(q_hbm, k_hbm, v_hbm, h_hbm, out_hbm, q_ref, k_ref, v_ref, h_ref, out_ref, sems):
    copies = fetch(((k_hbm, k_ref), (q_hbm, q_ref), (v_hbm, v_ref), (h_hbm, h_ref)), sems)
    rows = q_ref.shape[0]
    left = left_lanes(rows)
    for at, (first_ref, second_ref) in enumerate(((k_ref, q_ref), (v_ref, h_ref))):
        copies[2 * at].wait()
        copies[2 * at + 1].wait()
        for peer in range(out_ref.shape[0]):
            lanes = slice(LANES * (peer // 2), LANES * (peer // 2) + LANES)
            first = first_ref[:, lanes].astype(F32)
            second = second_ref[:, lanes].astype(F32)
            if peer % 2 == 0:
                both = jnp.where(left, first, other_half(second))
            else:
                both = jnp.where(left, other_half(first), second)
            out_ref[peer, at] = both.astype(BF16)
    finish(fetch(((out_ref, out_hbm),), sems))


def fold_rows(block):
    half = block.shape[0] // 2
    return jnp.where(left_lanes(half), block[:half], other_half(block[half:]))


def unfold_rows(folds):
    blocks, half, _ = folds.shape
    turned = pltpu.roll(folds, HALF, 2)
    left = lax.broadcasted_iota(jnp.int32, folds.shape, 2) < HALF
    both = [jnp.where(left, folds, turned), jnp.where(left, turned, folds)]
    return jnp.concatenate(both, axis=1).reshape(blocks * 2 * half, LANES)


def column_parts(w_hbm, w_ref, order, mine, sems):
    width = w_ref.shape[2]
    places = [pl.multiple_of((mine ^ mask) * width, width) for mask in order]
    return fetch(
        [(w_hbm.at[:, pl.ds(at, width)], w_ref.at[n]) for n, at in enumerate(places)], sems
    )


def grad_gated_kernel(
    ids_ref, c0_hbm, c1_hbm, c2_hbm, c3_hbm, w_hbm, after_ref, send_hbm,
    c0_ref, c1_ref, c2_ref, c3_ref, w_ref, send_ref, cot_sems, sems,
):
    mine = ids_ref[1]
    cots = (c0_ref, c1_ref, c2_ref, c3_ref)
    loads = fetch(zip((c0_hbm, c1_hbm, c2_hbm, c3_hbm), cots), cot_sems)
    copies = column_parts(w_hbm, w_ref, range(4), mine, sems)
    rows = c0_ref.shape[0]
    for mask, part_ref in enumerate(cots):
        loads[mask].wait()
        for half in range(2):
            at = pl.multiple_of(half * 4 * LANES + mine * LANES, LANES)
            turned = part_ref[:, pl.ds(at, LANES)].astype(F32).T
            send_ref[2 * (mine ^ mask) + half, rows // 2 :] = turned.astype(BF16)
    total = None
    for mask, part_ref in enumerate(cots):
        copies[mask].wait()
        term = lax.dot_general(
            part_ref[...], w_ref[mask], (((1,), (1,)), ((), ())), preferred_element_type=F32
        )
        total = term if total is None else total + term
    for peer in range(send_ref.shape[0]):
        tile = total[:, LANES * (peer // 2) : LANES * (peer // 2) + LANES]
        if peer % 2 == 1:
            tile = other_half(tile)
        send_ref[peer, : rows // 2] = fold_rows(tile).astype(BF16)
    finish(fetch(((send_ref, send_hbm),), sems))


def forward_kernel(
    moved_hbm, fwd_hbm, inv_hbm, after_hbm, prm_ref,
    send_hbm, kqs_hbm, vhs_hbm, mq_hbm, spec_hbm,
    moved_ref, fwd_ref, inv_ref, send_ref, kqs_ref, vhs_ref, mq_ref, spec_ref,
    signal_ref, y_ref, sems, out_sems,
):
    copies = fetch(((moved_hbm, moved_ref), (fwd_hbm, fwd_ref), (inv_hbm, inv_ref)), sems)
    peers, _, rows, _ = moved_ref.shape
    size = peers * rows
    left = left_lanes(size)
    copies[0].wait()
    kq = moved_ref[:, 0].reshape(size, LANES).astype(F32)
    vh = moved_ref[:, 1].reshape(size, LANES).astype(F32)
    kqs = sum(prm_ref[j : j + 1] * earlier_rows(kq, j) for j in range(3))
    vhs = sum(prm_ref[3 + j : 4 + j] * earlier_rows(vh, j) for j in range(3))
    kqs_ref[...] = kqs
    vhs_ref[...] = vhs
    done = fetch(((kqs_ref, kqs_hbm), (vhs_ref, vhs_hbm)), out_sems)
    product = kqs * vhs
    signal_ref[...] = jnp.where(left, product, vhs)
    copies[1].wait()
    spectrum(fwd_ref, signal_ref, spec_ref)
    done += fetch(((spec_ref, spec_hbm),), out_sems.at[pl.ds(2, 1)])
    parts = [None] * 4
    for mirror in range(2):
        xc, xs = spec_ref[mirror], spec_ref[2 + mirror]
        hc, hs = other_half(xc), other_half(xs)
        parts[mirror] = xc * hc - xs * hs
        parts[2 + mirror] = xc * hs + xs * hc
    copies[2].wait()
    from_spectrum(inv_ref, parts, y_ref)
    both_product = jnp.where(left, product, other_half(product))
    mixed = y_ref[...] + prm_ref[12:13] * both_product
    mq_ref[...] = jnp.where(left, mixed, kqs)
    gated = kqs * mixed
    left_rows = left_lanes(rows)
    for pair in range(peers // 2):
        first = gated[2 * rows * pair : 2 * rows * pair + rows]
        second = gated[2 * rows * pair + rows : 2 * rows * (pair + 1)]
        send_ref[pair] = jnp.where(left_rows, other_half(first), second).astype(BF16)
    done += fetch(((mq_ref, mq_hbm), (send_ref, send_hbm)), out_sems.at[pl.ds(3, 2)])
    finish(done)


def project_kernel(ids_ref, *refs):
    gates = refs[:8]
    w_hbm, keep_hbm, *send_hbm = refs[8:13]
    gate_ref, w_ref, keep_ref, *send_ref = refs[13:19]
    gated_ref, gate_sems, sems = refs[19:]
    own_row, mine = ids_ref[0], ids_ref[1]
    loads = fetch(
        [(gate.at[own_row // 2], gate_ref.at[at]) for at, gate in enumerate(gates)], gate_sems
    )
    order = (2, 3, 1, 0)
    copies = column_parts(w_hbm, w_ref, order, mine, sems)
    left = left_lanes(gate_ref.shape[1])
    odd = own_row % 2 == 1
    finish(loads)
    for pair in range(len(gates) // 2):
        one = gate_ref[2 * pair].astype(F32)
        two = gate_ref[2 * pair + 1].astype(F32)
        even_rows = jnp.where(left, one, other_half(two))
        odd_rows = jnp.where(left, other_half(two), one)
        lanes = pl.ds(pl.multiple_of(((own_row // 2) ^ pair) * LANES, LANES), LANES)
        gated_ref[:, lanes] = jnp.where(odd, odd_rows, even_rows).astype(BF16)
    gated = gated_ref[...]
    done = []
    for n, mask in enumerate(order):
        copies[n].wait()
        part = jnp.dot(gated, w_ref[n], preferred_element_type=F32)
        if mask:
            send_ref[mask - 1][...] = part.astype(BF16)
            target = (send_ref[mask - 1], send_hbm[mask - 1])
        else:
            keep_ref[...] = part
            target = (keep_ref, keep_hbm)
        done += fetch((target,), gate_sems.at[pl.ds(n, 1)])
    finish(done)


def backward_kernel(
    moved_hbm, mq_hbm, spec_hbm, kqs_hbm, vhs_hbm, streams_hbm, fwd_hbm, inv_hbm, prm_ref,
    send_hbm,
    moved_ref, mq_ref, spec_ref, kqs_ref, vhs_ref, streams_ref, fwd_ref, inv_ref, send_ref,
    signal_ref, mspec_ref, back_ref, sems,
):
    copies = fetch(
        (
            (moved_hbm.at[:, pl.ds(0, moved_ref.shape[1])], moved_ref),
            (mq_hbm, mq_ref),
            (fwd_hbm, fwd_ref),
            (spec_hbm, spec_ref),
            (inv_hbm, inv_ref),
            (kqs_hbm, kqs_ref),
            (vhs_hbm, vhs_ref),
            (streams_hbm, streams_ref),
        ),
        sems,
    )
    peers, _, rows, _ = streams_ref.shape
    size = peers * rows
    left = left_lanes(size)
    finish(copies[:2])
    z = unfold_rows(moved_ref[...].astype(F32)) * mq_ref[...]
    grad_mixed = jnp.where(left, other_half(z), z)
    signal_ref[...] = grad_mixed
    copies[2].wait()
    spectrum(fwd_ref, signal_ref, mspec_ref)
    copies[3].wait()
    parts = [None] * 4
    for mirror in range(2):
        xc, xs = spec_ref[mirror], spec_ref[2 + mirror]
        mc, ms = mspec_ref[mirror], mspec_ref[2 + mirror]
        parts[mirror] = xc * mc + xs * ms
        parts[2 + mirror] = xc * ms - xs * mc
    copies[4].wait()
    from_spectrum(inv_ref, parts, back_ref)
    finish(copies[5:])
    back = back_ref[...]
    kqs, vhs = kqs_ref[...], vhs_ref[...]
    grad_product = back + prm_ref[12:13] * grad_mixed
    grad_product = jnp.where(left, other_half(grad_product), grad_product)
    grad_kv = grad_product * jnp.where(left, vhs, other_half(kqs))
    grad_qf = jnp.where(left, z, other_half(back))
    kq = streams_ref[:, 0].reshape(size, LANES).astype(F32)
    vh = streams_ref[:, 1].reshape(size, LANES).astype(F32)
    raw_kv = jnp.where(left, kq, other_half(vh))
    raw_q = other_half(kq)
    out_kv = sum(prm_ref[6 + j : 7 + j] * later_rows(grad_kv, j) for j in range(3))
    out_qf = sum(prm_ref[9 + j : 10 + j] * later_rows(grad_qf, j) for j in range(3))
    sums = [jnp.sum(grad_kv * earlier_rows(raw_kv, j), axis=0, keepdims=True) for j in range(3)]
    sums += [jnp.sum(grad_qf * earlier_rows(raw_q, j), axis=0, keepdims=True) for j in range(3)]
    sums += [jnp.sum(grad_mixed * kqs * vhs, axis=0, keepdims=True)]
    sums += [jnp.zeros_like(sums[0])]
    small = jnp.concatenate(sums, axis=0)
    small_high = small.astype(BF16).astype(F32)
    small = jnp.concatenate([small_high, small - small_high], axis=0).astype(BF16)
    for peer in range(peers):
        at = slice(rows * peer, rows * peer + rows)
        send_ref[peer, :rows] = out_kv[at].astype(BF16)
        send_ref[peer, rows : 2 * rows] = out_qf[at].astype(BF16)
        send_ref[peer, 2 * rows :] = small
    finish(fetch(((send_ref, send_hbm),), sems))


def unpack_kernel(
    moved_hbm, q_hbm, k_hbm, v_hbm, f_hbm, short_ref, skip_ref,
    moved_ref, q_ref, k_ref, v_ref, f_ref, sems,
):
    finish(fetch(((moved_hbm, moved_ref),), sems))
    peers = moved_ref.shape[0]
    rows = q_ref.shape[0]
    left = left_lanes(rows)
    left_few = left_lanes(8)

    def merged(first, second, mask):
        return (
            jnp.where(mask, first, other_half(second)),
            jnp.where(mask, other_half(first), second),
        )

    tiles = range(peers // 2)
    for tile in tiles:
        lanes = slice(LANES * tile, LANES * tile + LANES)
        first, second = (moved_ref[2 * tile + n, :rows].astype(F32) for n in range(2))
        k_ref[:, lanes], v_ref[:, lanes] = merged(first, second, left)
    done = fetch(((k_ref, k_hbm), (v_ref, v_hbm)), sems)
    for tile in tiles:
        lanes = slice(LANES * tile, LANES * tile + LANES)
        first, second = (moved_ref[2 * tile + n, rows : 2 * rows].astype(F32) for n in range(2))
        q_ref[:, lanes], f_ref[:, lanes] = merged(first, second, left)
        few = [moved_ref[2 * tile + n, 2 * rows :].astype(F32) for n in range(2)]
        low, high = merged(few[0][:8] + few[0][8:], few[1][:8] + few[1][8:], left_few)
        short_ref[0, :, lanes] = low[3:6]
        short_ref[1, :, lanes] = low[0:3]
        short_ref[2, :, lanes] = high[0:3]
        skip_ref[:, lanes] = low[6:7]
    done += fetch(((q_ref, q_hbm), (f_ref, f_hbm)), sems.at[pl.ds(2, 2)])
    finish(done)


def grad_weight_kernel(ids_ref, *refs):
    cots, gates = refs[:4], refs[4:12]
    out_hbm, cot_ref, gate_ref, side_ref, total_ref, sems, out_sems = refs[12:]
    own_row, own = ids_ref[0], ids_ref[1]
    copies = fetch(
        [(cot, cot_ref.at[at]) for at, cot in enumerate(cots)]
        + [(gate, gate_ref.at[at]) for at, gate in enumerate(gates)],
        sems,
    )
    _, peers, high, wide = cot_ref.shape
    left = left_lanes(4 * high)
    odd = own_row % 2 == 1
    for mask in range(4):
        copies[mask].wait()
        for peer in range(peers):
            lanes = slice(wide * (peer // 2), wide * (peer // 2) + wide)
            side_ref[peer % 2, high * mask : high * mask + high, lanes] = cot_ref[mask, peer]
    done = []
    for pair in range(peers // 2):
        finish(copies[4 + 2 * pair : 6 + 2 * pair])
        found = []
        for at in (2 * pair, 2 * pair + 1):
            gate = gate_ref[at].reshape(peers // 2 * wide, LANES)
            found.append(
                [jnp.dot(side_ref[n], gate, preferred_element_type=F32) for n in range(2)]
            )
        (even_low, even_high), (odd_low, odd_high) = found
        even_sum = even_low + other_half(even_high)
        odd_sum = odd_low + other_half(odd_high)
        ahead = jnp.where(left, even_sum, other_half(odd_sum))
        behind = jnp.where(left, odd_sum, other_half(even_sum))
        tile = jnp.where(odd, behind, ahead)
        for mask in range(4):
            at = pl.ds(pl.multiple_of((own ^ mask) * high, high), high)
            total_ref[pair, at] = tile[high * mask : high * mask + high]
        lanes = pl.ds(pl.multiple_of(((own_row // 2) ^ pair) * LANES, LANES), LANES)
        done += fetch(
            ((total_ref.at[pair], out_hbm.at[:, lanes]),), out_sems.at[pl.ds(pair, 1)]
        )
    finish(done)


def call(
    kernel, outs, scalars, *arrays, small=(), small_outs=(), scratch=(), dmas=(8,)
):
    vmem = pl.BlockSpec(memory_space=pltpu.VMEM)
    smem = pl.BlockSpec(memory_space=pltpu.SMEM)
    hbm = pl.BlockSpec(memory_space=pltpu.HBM)
    return pl.pallas_call(
        kernel,
        out_shape=list(outs) + list(small_outs),
        in_specs=[smem] * len(scalars) + [hbm] * len(arrays) + [vmem] * len(small),
        out_specs=[hbm] * len(outs) + [vmem] * len(small_outs),
        scratch_shapes=[pltpu.VMEM(a.shape, a.dtype) for a in scratch]
        + [pltpu.SemaphoreType.DMA((count,)) for count in dmas],
        compiler_params=pltpu.CompilerParams(vmem_limit_bytes=LIMIT),
        cost_estimate=pl.CostEstimate(
            flops=1, bytes_accessed=1, transcendentals=0
        ),
        name=kernel.__name__.removesuffix("_kernel"),
    )(*scalars, *arrays, *small)


def shaped(shape, dtype):
    return jax.ShapeDtypeStruct(shape, dtype)


def gathered_pairs(block, axis):
    near = swap_bits(block, axis, 1)
    far = swap_bits(block, axis, 2)
    return [block, near, far, swap_bits(far, axis, 1)]


def gathered_first(block, axis):
    mask = lax.axis_size(axis) // 2
    return {0: block, mask: swap_bits(block, axis, mask), mask // 2: swap_bits(block, axis, mask // 2), 1: swap_bits(block, axis, 1)}


def gathered_rest(blocks, axis):
    top = lax.axis_size(axis) // 2
    mask = top // 2
    while mask:
        for at in list(blocks):
            if at % (2 * mask) == 0 and at | mask not in blocks:
                blocks[at | mask] = swap_bits(blocks[at], axis, mask)
        mask //= 2
    return [blocks[at] for at in range(len(blocks))]


def on_device_packed(
    query_proj, key_proj, value_proj, short_filter, long_filter, skip_gain, out_weight, cotangent
):
    peers = lax.axis_size("seq")
    rows, channels = query_proj.shape
    features = cotangent.shape[1]
    size = peers * rows
    seq_at, ch_at = lax.axis_index("seq"), lax.axis_index("ch")
    ids = jnp.stack([seq_at, ch_at]).astype(jnp.int32)
    forward_table, inverse_table = (jnp.asarray(table) for table in wave_tables(size))
    cots = gathered_pairs(cotangent, "ch")

    own_short = lax.dynamic_slice_in_dim(short_filter, seq_at * HALF, HALF, 2)
    own_skip = lax.dynamic_slice_in_dim(skip_gain, seq_at * HALF, HALF, 0)[None]
    unit = (lax.broadcasted_iota(jnp.int32, (3, HALF), 0) == 0).astype(F32)
    wq, wk, wv = own_short[0], own_short[1], own_short[2]
    prm = jnp.concatenate(
        [
            jnp.concatenate([wk, wv, wk, wq, own_skip], axis=0),
            jnp.concatenate([wq, unit, wv, unit, own_skip], axis=0),
        ],
        axis=1,
    )

    inputs = (query_proj, key_proj, value_proj, long_filter)
    packs = shaped((peers, 2, rows, LANES), BF16)
    (packed,) = call(pack_streams_kernel, [packs], [], *inputs, scratch=(*inputs, packs))
    streams = lax.all_to_all(packed, "seq", 0, 0, tiled=True)
    weight_room = shaped((4, channels, features), BF16)
    sent = shaped((peers, rows // 2 + rows, LANES), BF16)
    (sent_grad,) = call(
        grad_gated_kernel,
        [sent],
        [ids],
        *cots,
        out_weight,
        small=(prm,),
        scratch=(*cots, weight_room, sent),
        dmas=(4, 4),
    )
    moved_grad = lax.all_to_all(sent_grad, "seq", 0, 0, tiled=True)
    wide = shaped((size, LANES), F32)
    spectra = shaped((4, size // 2, LANES), F32)
    folds = shaped((peers // 2, rows, LANES), BF16)
    tables = (forward_table, inverse_table)
    results = [folds, wide, wide, wide, spectra]
    gated, kqs, vhs, mq, spec = call(
        forward_kernel,
        results,
        [],
        streams,
        *tables,
        sent_grad,
        small=(prm,),
        scratch=(packs, *tables, *results, wide, wide),
        dmas=(3, 5),
    )
    first_gates = gathered_first(gated, "seq")
    backs = shaped((peers, 2 * rows + 16, LANES), BF16)
    saved = (mq, spec, kqs, vhs, streams, *tables)
    (back,) = call(
        backward_kernel,
        [backs],
        [],
        moved_grad,
        *saved,
        small=(prm,),
        scratch=(
            shaped((peers, rows // 2, LANES), BF16), *saved, backs, wide, spectra, wide
        ),
    )
    cot_parts = gathered_pairs(moved_grad[:, rows // 2 :], "ch")
    back, first_gates = lax.optimization_barrier((back, first_gates))
    gates = gathered_rest(first_gates, "seq")
    back, gates = lax.optimization_barrier((back, gates))
    returned = lax.all_to_all(back, "seq", 0, 0, tiled=True)
    sums = [shaped((rows, features), F32)] + [shaped((rows, features), BF16)] * 3
    keep, *away = call(
        project_kernel,
        sums,
        [ids],
        *gates,
        out_weight,
        scratch=(
            shaped((peers, rows, LANES), BF16),
            weight_room,
            *sums,
            shaped((rows, channels), BF16),
        ),
        dmas=(8, 4),
    )
    shares = [swap_bits(part, "ch", mask) for mask, part in enumerate(away, 1)]
    plain = shaped((rows, channels), F32)
    grad_query, grad_key, grad_value, grad_filter, grad_short, grad_skip = call(
        unpack_kernel,
        [plain] * 4,
        [],
        returned,
        small_outs=[shaped((3, 3, channels), F32), shaped((1, channels), F32)],
        scratch=(backs, plain, plain, plain, plain),
    )
    (grad_w_out_t,) = call(
        grad_weight_kernel,
        [shaped((4 * LANES, channels), F32)],
        [ids],
        *cot_parts,
        *gates,
        scratch=(
            shaped((4, peers, LANES, rows), BF16),
            shaped((peers, peers // 2, rows, LANES), BF16),
            shaped((2, 4 * LANES, peers // 2 * rows), BF16),
            shaped((peers // 2, 4 * LANES, LANES), F32),
        ),
        dmas=(12, 4),
    )
    shares, grad_w_out_t, grad_filter = lax.optimization_barrier(
        (shares, grad_w_out_t, grad_filter)
    )
    for part in shares:
        keep = keep + part.astype(F32)
    layer_out = keep.astype(BF16)
    return (
        layer_out,
        grad_query,
        grad_key,
        grad_value,
        grad_short,
        grad_filter,
        grad_skip[0],
        grad_w_out_t,
    )


def solution(mesh):
    in_specs = (
        P("seq", "ch"),
        P("seq", "ch"),
        P("seq", "ch"),
        P(None, None, "ch"),
        P("seq", "ch"),
        P("ch"),
        P("ch", None),
        P("seq", "ch"),
    )
    out_specs = (
        P("seq", "ch"),
        P("seq", "ch"),
        P("seq", "ch"),
        P("seq", "ch"),
        P(None, None, "ch"),
        P("seq", "ch"),
        P("ch"),
        P("seq", "ch"),
    )
    split = dict(mesh.shape)

    def whole(*arrays):
        rows = arrays[0].shape[0] // split["seq"]
        channels = arrays[0].shape[1] // split["ch"]
        features = arrays[7].shape[1]
        packs = (
            split["ch"] == 4
            and channels == HALF * split["seq"]
            and features == 4 * LANES * split["seq"]
            and arrays[0].shape[0] <= 1024
            and rows % 16 == 0
            and arrays[3].shape[1] == 3
        )
        body = on_device_packed if packs else on_device
        return jax.shard_map(
            body,
            mesh=mesh,
            in_specs=in_specs,
            out_specs=out_specs,
            check_vma=False,
        )(*arrays)

    return whole
```

```python
import functools
import math

import jax
import jax.numpy as jnp
import ml_dtypes
import numpy as np
from jax import lax
from jax.experimental import pallas as pl
from jax.experimental.pallas import tpu as pltpu
from jax.sharding import PartitionSpec as P

exact_mode = lax.Precision.HIGHEST


def from_behind(shard, axis, by):
    size = lax.axis_size(axis)
    pairs = [(i, i + by) for i in range(size) if 0 <= i + by < size]
    return lax.ppermute(shard, axis, pairs)


def as_sent(shard):

    def short(part):
        return part.astype(jnp.bfloat16) if part.dtype == jnp.float32 else part

    return jax.tree.map(short, shard)


def tables(rows_out, cols_in, period):
    row_index = lax.broadcasted_iota(jnp.int32, (rows_out, cols_in), 0)
    col_index = lax.broadcasted_iota(jnp.int32, (rows_out, cols_in), 1)
    phase_angle = (row_index * col_index % period).astype(jnp.float32) * (2.0 * math.pi / period)
    return (jnp.cos(phase_angle), jnp.sin(phase_angle))


def along_rows(factor, values):
    return jnp.tensordot(factor, values, axes=1, precision=exact_mode)


def rows_spectrum(signal, basis_pair):
    return (along_rows(basis_pair[0], signal), -along_rows(basis_pair[1], signal))


def rows_inverse(complex_pair, basis_pair):
    total = along_rows(basis_pair[0], complex_pair[0]) - along_rows(basis_pair[1], complex_pair[1])
    return total / basis_pair[0].shape[1]


def block_forward(complex_pair, basis_pair):
    cosine_part, sine_part = basis_pair
    real_part = along_rows(cosine_part, complex_pair[0]) + along_rows(sine_part, complex_pair[1])
    imag_part = along_rows(cosine_part, complex_pair[1]) - along_rows(sine_part, complex_pair[0])
    return (real_part, imag_part)


def block_inverse(complex_pair, basis_pair):
    cosine_part, sine_part = basis_pair
    norming = 1.0 / cosine_part.shape[1]
    real_part = along_rows(cosine_part, complex_pair[0]) - along_rows(sine_part, complex_pair[1])
    imag_part = along_rows(cosine_part, complex_pair[1]) + along_rows(sine_part, complex_pair[0])
    return (real_part * norming, imag_part * norming)


def complex_product(first_pair, second_pair):
    return (
        first_pair[0] * second_pair[0] - first_pair[1] * second_pair[1],
        first_pair[0] * second_pair[1] + first_pair[1] * second_pair[0],
    )


def conj_product(first_pair, second_pair):
    return (
        first_pair[0] * second_pair[0] + first_pair[1] * second_pair[1],
        first_pair[0] * second_pair[1] - first_pair[1] * second_pair[0],
    )


def on_device(
    query_proj, key_proj, value_proj, short_filter, long_filter, skip_gain, out_weight, cotangent
):
    block_rows = query_proj.shape[0]
    tap_count = short_filter.shape[1]
    block_count = lax.axis_size("seq")
    streams = jnp.stack([query_proj, key_proj, value_proj])
    earlier = from_behind(streams[:, block_rows - (tap_count - 1) :], "seq", 1)
    extended = jnp.concatenate([earlier, streams], axis=1).astype(jnp.float32)
    shifted = [
        extended[:, tap_count - 1 - offset : tap_count - 1 - offset + block_rows]
        for offset in range(tap_count)
    ]
    filtered = sum(
        (short_filter[:, offset][:, None, :] * shifted[offset] for offset in range(tap_count))
    )
    query_short, key_short, value_short = (filtered[0], filtered[1], filtered[2])
    product = key_short * value_short
    forward_basis = tables(2 * block_rows, block_rows, 2 * block_rows)
    full_basis = tables(2 * block_rows, 2 * block_rows, 2 * block_rows)
    half_basis = tables(block_rows, 2 * block_rows, 2 * block_rows)
    block_basis = tables(2 * block_count, block_count, 2 * block_count)
    return_basis = tables(block_count, 2 * block_count, 2 * block_count)
    input_pair = rows_spectrum(product, forward_basis)
    filter_pair = rows_spectrum(long_filter, forward_basis)
    moved_data = (
        lax.all_to_all(input_pair[0][None], "seq", split_axis=1, concat_axis=0, tiled=True),
        lax.all_to_all(input_pair[1][None], "seq", split_axis=1, concat_axis=0, tiled=True),
        lax.all_to_all(filter_pair[0][None], "seq", split_axis=1, concat_axis=0, tiled=True),
        lax.all_to_all(filter_pair[1][None], "seq", split_axis=1, concat_axis=0, tiled=True),
    )
    input_spectrum = block_forward((moved_data[0], moved_data[1]), block_basis)
    filter_spectrum = block_forward((moved_data[2], moved_data[3]), block_basis)
    inverse_pair = block_inverse(complex_product(filter_spectrum, input_spectrum), return_basis)
    returned = (
        lax.all_to_all(inverse_pair[0], "seq", split_axis=0, concat_axis=1, tiled=True),
        lax.all_to_all(inverse_pair[1], "seq", split_axis=0, concat_axis=1, tiled=True),
    )
    folded = rows_inverse((returned[0][0], returned[1][0]), full_basis)
    carried = from_behind(folded[block_rows:], "seq", 1)
    convolved = folded[:block_rows] + carried
    mixed_seq = convolved + skip_gain * product
    gated_values = (query_short * mixed_seq).astype(jnp.bfloat16)
    partial_value = jnp.dot(gated_values, out_weight, preferred_element_type=jnp.float32)
    layer_out = lax.psum_scatter(partial_value, "ch", scatter_dimension=1, tiled=True).astype(
        jnp.bfloat16
    )
    full_cotangent = lax.all_gather(cotangent, "ch", axis=1, tiled=True)
    grad_gated = lax.dot_general(
        full_cotangent, out_weight, (((1,), (1,)), ((), ())), preferred_element_type=jnp.float32
    )
    grad_w_out_t = lax.psum_scatter(
        lax.dot_general(
            full_cotangent,
            gated_values,
            (((0,), (0,)), ((), ())),
            preferred_element_type=jnp.float32,
        ),
        "seq",
        scatter_dimension=0,
        tiled=True,
    )
    grad_mixed = grad_gated * query_short
    grad_query_short = grad_gated * mixed_seq
    following = from_behind(grad_mixed.astype(jnp.bfloat16), "seq", -1).astype(grad_mixed.dtype)
    spread = jnp.concatenate([grad_mixed, following], axis=0)
    grad_pair = rows_spectrum(spread, full_basis)
    moved_grad = (
        lax.all_to_all(
            grad_pair[0][None].astype(jnp.bfloat16), "seq", split_axis=1, concat_axis=0, tiled=True
        ).astype(jnp.float32),
        lax.all_to_all(
            grad_pair[1][None].astype(jnp.bfloat16), "seq", split_axis=1, concat_axis=0, tiled=True
        ).astype(jnp.float32),
    )
    grad_spectrum = block_forward(moved_grad, block_basis)
    input_back = block_inverse(conj_product(filter_spectrum, grad_spectrum), return_basis)
    filter_back = block_inverse(conj_product(input_spectrum, grad_spectrum), return_basis)
    returned_grad = (
        lax.all_to_all(as_sent(input_back[0]), "seq", split_axis=0, concat_axis=1, tiled=True),
        lax.all_to_all(as_sent(input_back[1]), "seq", split_axis=0, concat_axis=1, tiled=True),
        lax.all_to_all(as_sent(filter_back[0]), "seq", split_axis=0, concat_axis=1, tiled=True),
        lax.all_to_all(as_sent(filter_back[1]), "seq", split_axis=0, concat_axis=1, tiled=True),
    )
    conv_grad = rows_inverse((returned_grad[0][0], returned_grad[1][0]), half_basis)
    grad_filter = rows_inverse((returned_grad[2][0], returned_grad[3][0]), half_basis)
    grad_product = conv_grad + skip_gain * grad_mixed
    grad_streams = jnp.stack(
        [grad_query_short, grad_product * value_short, grad_product * key_short]
    )
    later_rows = from_behind(grad_streams[:, : tap_count - 1], "seq", -1)
    padded_grad = jnp.concatenate([grad_streams, later_rows], axis=1)
    grad_inputs = sum(
        (
            short_filter[:, offset][:, None, :] * padded_grad[:, offset : offset + block_rows]
            for offset in range(tap_count)
        )
    )
    short_terms = jnp.stack(
        [jnp.sum(grad_streams * shifted[offset], axis=1) for offset in range(tap_count)], axis=1
    )
    skip_terms = jnp.sum(grad_mixed * product, axis=0)
    grad_short, grad_skip = lax.psum((short_terms, skip_terms), "seq")
    return (
        layer_out,
        grad_inputs[0],
        grad_inputs[1],
        grad_inputs[2],
        grad_short,
        grad_filter,
        grad_skip,
        grad_w_out_t,
    )


LANES = 128
HALF = 64
LIMIT = 63 * 2**20 + 2**19
F32 = jnp.float32
BF16 = jnp.bfloat16


def swap_bits(shard, axis, mask):
    size = lax.axis_size(axis)
    return lax.ppermute(shard, axis, [(i, i ^ mask) for i in range(size)])


@functools.lru_cache
def wave_tables(rows):
    half = rows // 2
    steps = np.outer(2 * np.arange(half) + 1, np.arange(rows)) % (4 * rows)
    angle = steps * (math.pi / (2 * rows))
    waves = np.concatenate([np.cos(angle), np.sin(angle)], axis=0)
    split = np.stack([waves[:, 0::2], waves[:, 1::2]])
    inverse = np.swapaxes(split, 1, 2) / rows
    return split.astype(ml_dtypes.bfloat16), inverse.astype(ml_dtypes.bfloat16)


def left_lanes(rows):
    return lax.broadcasted_iota(jnp.int32, (rows, LANES), 1) < HALF


def other_half(block):
    return pltpu.roll(block, HALF, 1)


def earlier_rows(block, by):
    if by == 0:
        return block
    row = lax.broadcasted_iota(jnp.int32, block.shape, 0)
    return jnp.where(row >= by, pltpu.roll(block, by, 0), 0.0)


def later_rows(block, by):
    if by == 0:
        return block
    size = block.shape[0]
    row = lax.broadcasted_iota(jnp.int32, block.shape, 0)
    return jnp.where(row < size - by, pltpu.roll(block, size - by, 0), 0.0)


def spectrum(table_ref, signal_ref, out_ref):
    half = table_ref.shape[2]
    quarter = 256
    even = signal_ref[pl.ds(0, half, stride=2)].astype(BF16)
    odd = signal_ref[pl.ds(1, half, stride=2)].astype(BF16)
    for start in range(0, 2 * half, quarter):
        at = slice(start, start + quarter)
        first = jnp.dot(table_ref[0, at], even, preferred_element_type=F32)
        second = jnp.dot(table_ref[1, at], odd, preferred_element_type=F32)
        kind, row = (0, start) if start < half else (2, start - half)
        out_ref[kind, row : row + quarter] = first + second
        mirrored = first - second if kind == 0 else second - first
        out_ref[kind + 1, row : row + quarter] = mirrored


def from_spectrum(table_ref, parts, out_ref):
    half = table_ref.shape[1]
    quarter = 256
    cosine, cosine_mirror, sine, sine_mirror = parts
    even = jnp.concatenate([cosine + cosine_mirror, sine - sine_mirror], axis=0).astype(BF16)
    odd = jnp.concatenate([cosine - cosine_mirror, sine + sine_mirror], axis=0).astype(BF16)
    for side, operand in enumerate((even, odd)):
        for start in range(0, half, quarter):
            out_ref[pl.ds(2 * start + side, quarter, stride=2)] = jnp.dot(
                table_ref[side, start : start + quarter], operand, preferred_element_type=F32
            )


def fetch(pairs, sems):
    copies = [
        pltpu.make_async_copy(source, target, sems.at[at])
        for at, (source, target) in enumerate(pairs)
    ]
    for copy in copies:
        copy.start()
    return copies


def finish(copies):
    for copy in copies:
        copy.wait()


def pack_streams_kernel(q_hbm, k_hbm, v_hbm, h_hbm, out_hbm, q_ref, k_ref, v_ref, h_ref, out_ref, sems):
    copies = fetch(((k_hbm, k_ref), (q_hbm, q_ref), (v_hbm, v_ref), (h_hbm, h_ref)), sems)
    rows = q_ref.shape[0]
    left = left_lanes(rows)
    for at, (first_ref, second_ref) in enumerate(((k_ref, q_ref), (v_ref, h_ref))):
        copies[2 * at].wait()
        copies[2 * at + 1].wait()
        for peer in range(out_ref.shape[0]):
            lanes = slice(LANES * (peer // 2), LANES * (peer // 2) + LANES)
            first = first_ref[:, lanes].astype(F32)
            second = second_ref[:, lanes].astype(F32)
            if peer % 2 == 0:
                both = jnp.where(left, first, other_half(second))
            else:
                both = jnp.where(left, other_half(first), second)
            out_ref[peer, at] = both.astype(BF16)
    finish(fetch(((out_ref, out_hbm),), sems))


def fold_rows(block):
    half = block.shape[0] // 2
    return jnp.where(left_lanes(half), block[:half], other_half(block[half:]))


def unfold_rows(folds):
    blocks, half, _ = folds.shape
    turned = pltpu.roll(folds, HALF, 2)
    left = lax.broadcasted_iota(jnp.int32, folds.shape, 2) < HALF
    both = [jnp.where(left, folds, turned), jnp.where(left, turned, folds)]
    return jnp.concatenate(both, axis=1).reshape(blocks * 2 * half, LANES)


def column_parts(w_hbm, w_ref, order, mine, sems):
    width = w_ref.shape[2]
    places = [pl.multiple_of((mine ^ mask) * width, width) for mask in order]
    return fetch(
        [(w_hbm.at[:, pl.ds(at, width)], w_ref.at[n]) for n, at in enumerate(places)], sems
    )


def grad_gated_kernel(
    ids_ref, c0_hbm, c1_hbm, c2_hbm, c3_hbm, w_hbm, after_ref, send_hbm,
    c0_ref, c1_ref, c2_ref, c3_ref, w_ref, send_ref, cot_sems, sems,
):
    mine = ids_ref[1]
    cots = (c0_ref, c1_ref, c2_ref, c3_ref)
    loads = fetch(zip((c0_hbm, c1_hbm, c2_hbm, c3_hbm), cots), cot_sems)
    copies = column_parts(w_hbm, w_ref, range(4), mine, sems)
    rows = c0_ref.shape[0]
    for mask, part_ref in enumerate(cots):
        loads[mask].wait()
        for half in range(2):
            at = pl.multiple_of(half * 4 * LANES + mine * LANES, LANES)
            turned = part_ref[:, pl.ds(at, LANES)].astype(F32).T
            send_ref[2 * (mine ^ mask) + half, rows // 2 :] = turned.astype(BF16)
    total = None
    for mask, part_ref in enumerate(cots):
        copies[mask].wait()
        term = lax.dot_general(
            part_ref[...], w_ref[mask], (((1,), (1,)), ((), ())), preferred_element_type=F32
        )
        total = term if total is None else total + term
    for peer in range(send_ref.shape[0]):
        tile = total[:, LANES * (peer // 2) : LANES * (peer // 2) + LANES]
        if peer % 2 == 1:
            tile = other_half(tile)
        send_ref[peer, : rows // 2] = fold_rows(tile).astype(BF16)
    finish(fetch(((send_ref, send_hbm),), sems))


def forward_kernel(
    moved_hbm, fwd_hbm, inv_hbm, after_hbm, prm_ref,
    send_hbm, kqs_hbm, vhs_hbm, mq_hbm, spec_hbm,
    moved_ref, fwd_ref, inv_ref, send_ref, kqs_ref, vhs_ref, mq_ref, spec_ref,
    signal_ref, y_ref, sems, out_sems,
):
    copies = fetch(((moved_hbm, moved_ref), (fwd_hbm, fwd_ref), (inv_hbm, inv_ref)), sems)
    peers, _, rows, _ = moved_ref.shape
    size = peers * rows
    left = left_lanes(size)
    copies[0].wait()
    kq = moved_ref[:, 0].reshape(size, LANES).astype(F32)
    vh = moved_ref[:, 1].reshape(size, LANES).astype(F32)
    kqs = sum(prm_ref[j : j + 1] * earlier_rows(kq, j) for j in range(3))
    vhs = sum(prm_ref[3 + j : 4 + j] * earlier_rows(vh, j) for j in range(3))
    kqs_ref[...] = kqs
    vhs_ref[...] = vhs
    done = fetch(((kqs_ref, kqs_hbm), (vhs_ref, vhs_hbm)), out_sems)
    product = kqs * vhs
    signal_ref[...] = jnp.where(left, product, vhs)
    copies[1].wait()
    spectrum(fwd_ref, signal_ref, spec_ref)
    done += fetch(((spec_ref, spec_hbm),), out_sems.at[pl.ds(2, 1)])
    parts = [None] * 4
    for mirror in range(2):
        xc, xs = spec_ref[mirror], spec_ref[2 + mirror]
        hc, hs = other_half(xc), other_half(xs)
        parts[mirror] = xc * hc - xs * hs
        parts[2 + mirror] = xc * hs + xs * hc
    copies[2].wait()
    from_spectrum(inv_ref, parts, y_ref)
    both_product = jnp.where(left, product, other_half(product))
    mixed = y_ref[...] + prm_ref[12:13] * both_product
    mq_ref[...] = jnp.where(left, mixed, kqs)
    gated = kqs * mixed
    left_rows = left_lanes(rows)
    for pair in range(peers // 2):
        first = gated[2 * rows * pair : 2 * rows * pair + rows]
        second = gated[2 * rows * pair + rows : 2 * rows * (pair + 1)]
        send_ref[pair] = jnp.where(left_rows, other_half(first), second).astype(BF16)
    done += fetch(((mq_ref, mq_hbm), (send_ref, send_hbm)), out_sems.at[pl.ds(3, 2)])
    finish(done)


def project_kernel(ids_ref, *refs):
    gates = refs[:16]
    w_hbm, other_hbm, keep_hbm, away_hbm = refs[16:20]
    gate_ref, w_ref, keep_ref, away_ref, gated_ref, gate_sems, sems = refs[20:]
    own_row, mine = ids_ref[0], ids_ref[1]
    loads = fetch(
        [(gate.at[own_row // 2], gate_ref.at[at]) for at, gate in enumerate(gates)], gate_sems
    )
    width = keep_ref.shape[1]
    copies = []
    for n, (hbm, mask) in enumerate(((w_hbm, 2), (other_hbm, 2), (w_hbm, 0), (other_hbm, 0))):
        at = pl.multiple_of((mine ^ mask) * width, width)
        copies += fetch(((hbm.at[:, pl.ds(at, width)], w_ref.at[n]),), sems.at[pl.ds(n, 1)])
    left = left_lanes(gate_ref.shape[1])
    odd = own_row % 2 == 1
    for side in range(2):
        finish(loads[8 * side : 8 * side + 8])
        for pair in range(4):
            one = gate_ref[8 * side + 2 * pair].astype(F32)
            two = gate_ref[8 * side + 2 * pair + 1].astype(F32)
            even_rows = jnp.where(left, one, other_half(two))
            odd_rows = jnp.where(left, other_half(two), one)
            lanes = pl.ds(pl.multiple_of(((own_row // 2) ^ pair) * LANES, LANES), LANES)
            gated_ref[side, :, lanes] = jnp.where(odd, odd_rows, even_rows).astype(BF16)
    done = []
    for n, (out_ref, out_hbm) in enumerate(((away_ref, away_hbm), (keep_ref, keep_hbm))):
        total = None
        for side in range(2):
            copies[2 * n + side].wait()
            part = jnp.dot(gated_ref[side], w_ref[2 * n + side], preferred_element_type=F32)
            total = part if total is None else total + part
        out_ref[...] = total.astype(out_ref.dtype)
        done += fetch(((out_ref, out_hbm),), gate_sems.at[pl.ds(n, 1)])
    finish(done)


def backward_kernel(
    moved_hbm, mq_hbm, spec_hbm, kqs_hbm, vhs_hbm, streams_hbm, fwd_hbm, inv_hbm, prm_ref,
    send_hbm,
    moved_ref, mq_ref, spec_ref, kqs_ref, vhs_ref, streams_ref, fwd_ref, inv_ref, send_ref,
    signal_ref, mspec_ref, back_ref, sems,
):
    copies = fetch(
        (
            (moved_hbm.at[:, pl.ds(0, moved_ref.shape[1])], moved_ref),
            (mq_hbm, mq_ref),
            (fwd_hbm, fwd_ref),
            (spec_hbm, spec_ref),
            (inv_hbm, inv_ref),
            (kqs_hbm, kqs_ref),
            (vhs_hbm, vhs_ref),
            (streams_hbm, streams_ref),
        ),
        sems,
    )
    peers, _, rows, _ = streams_ref.shape
    size = peers * rows
    left = left_lanes(size)
    finish(copies[:2])
    z = unfold_rows(moved_ref[...].astype(F32)) * mq_ref[...]
    grad_mixed = jnp.where(left, other_half(z), z)
    signal_ref[...] = grad_mixed
    copies[2].wait()
    spectrum(fwd_ref, signal_ref, mspec_ref)
    copies[3].wait()
    parts = [None] * 4
    for mirror in range(2):
        xc, xs = spec_ref[mirror], spec_ref[2 + mirror]
        mc, ms = mspec_ref[mirror], mspec_ref[2 + mirror]
        parts[mirror] = xc * mc + xs * ms
        parts[2 + mirror] = xc * ms - xs * mc
    copies[4].wait()
    from_spectrum(inv_ref, parts, back_ref)
    finish(copies[5:])
    back = back_ref[...]
    kqs, vhs = kqs_ref[...], vhs_ref[...]
    grad_product = back + prm_ref[12:13] * grad_mixed
    grad_product = jnp.where(left, other_half(grad_product), grad_product)
    grad_kv = grad_product * jnp.where(left, vhs, other_half(kqs))
    grad_qf = jnp.where(left, z, other_half(back))
    kq = streams_ref[:, 0].reshape(size, LANES).astype(F32)
    vh = streams_ref[:, 1].reshape(size, LANES).astype(F32)
    raw_kv = jnp.where(left, kq, other_half(vh))
    raw_q = other_half(kq)
    out_kv = sum(prm_ref[6 + j : 7 + j] * later_rows(grad_kv, j) for j in range(3))
    out_qf = sum(prm_ref[9 + j : 10 + j] * later_rows(grad_qf, j) for j in range(3))
    sums = [jnp.sum(grad_kv * earlier_rows(raw_kv, j), axis=0, keepdims=True) for j in range(3)]
    sums += [jnp.sum(grad_qf * earlier_rows(raw_q, j), axis=0, keepdims=True) for j in range(3)]
    sums += [jnp.sum(grad_mixed * kqs * vhs, axis=0, keepdims=True)]
    sums += [jnp.zeros_like(sums[0])]
    small = jnp.concatenate(sums, axis=0)
    small_high = small.astype(BF16).astype(F32)
    small = jnp.concatenate([small_high, small - small_high], axis=0).astype(BF16)
    for peer in range(peers):
        at = slice(rows * peer, rows * peer + rows)
        send_ref[peer, :rows] = out_kv[at].astype(BF16)
        send_ref[peer, rows : 2 * rows] = out_qf[at].astype(BF16)
        send_ref[peer, 2 * rows :] = small
    finish(fetch(((send_ref, send_hbm),), sems))


def unpack_kernel(
    moved_hbm, q_hbm, k_hbm, v_hbm, f_hbm, short_ref, skip_ref,
    moved_ref, q_ref, k_ref, v_ref, f_ref, sems,
):
    finish(fetch(((moved_hbm, moved_ref),), sems))
    peers = moved_ref.shape[0]
    rows = q_ref.shape[0]
    left = left_lanes(rows)
    left_few = left_lanes(8)

    def merged(first, second, mask):
        return (
            jnp.where(mask, first, other_half(second)),
            jnp.where(mask, other_half(first), second),
        )

    tiles = range(peers // 2)
    for tile in tiles:
        lanes = slice(LANES * tile, LANES * tile + LANES)
        first, second = (moved_ref[2 * tile + n, :rows].astype(F32) for n in range(2))
        k_ref[:, lanes], v_ref[:, lanes] = merged(first, second, left)
    done = fetch(((k_ref, k_hbm), (v_ref, v_hbm)), sems)
    for tile in tiles:
        lanes = slice(LANES * tile, LANES * tile + LANES)
        first, second = (moved_ref[2 * tile + n, rows : 2 * rows].astype(F32) for n in range(2))
        q_ref[:, lanes], f_ref[:, lanes] = merged(first, second, left)
        few = [moved_ref[2 * tile + n, 2 * rows :].astype(F32) for n in range(2)]
        low, high = merged(few[0][:8] + few[0][8:], few[1][:8] + few[1][8:], left_few)
        short_ref[0, :, lanes] = low[3:6]
        short_ref[1, :, lanes] = low[0:3]
        short_ref[2, :, lanes] = high[0:3]
        skip_ref[:, lanes] = low[6:7]
    done += fetch(((q_ref, q_hbm), (f_ref, f_hbm)), sems.at[pl.ds(2, 2)])
    finish(done)


def grad_weight_kernel(ids_ref, *refs):
    cots, gates = refs[:4], refs[4:12]
    out_hbm, cot_ref, gate_ref, side_ref, total_ref, sems, out_sems = refs[12:]
    own_row, own = ids_ref[0], ids_ref[1]
    lanes = [pl.ds(LANES * half, LANES) for half in range(2)]
    copies = fetch(
        [(cot, cot_ref.at[at]) for at, cot in enumerate(cots)]
        + [
            (gate, gate_ref.at[at // 2, :, :, lanes[at % 2]]) for at, gate in enumerate(gates)
        ],
        sems,
    )
    _, peers, high, wide = cot_ref.shape
    left = left_lanes(4 * high)
    odd = own_row % 2 == 1
    for mask in range(4):
        copies[mask].wait()
        for peer in range(peers):
            at = slice(wide * (peer // 2), wide * (peer // 2) + wide)
            side_ref[peer % 2, high * mask : high * mask + high, at] = cot_ref[mask, peer]
    done = []
    for pair in range(peers // 2):
        finish(copies[4 + 2 * pair : 6 + 2 * pair])
        gate = gate_ref[pair].reshape(peers // 2 * wide, 2 * LANES)
        low = jnp.dot(side_ref[0], gate, preferred_element_type=F32)
        high_part = jnp.dot(side_ref[1], gate, preferred_element_type=F32)
        even_sum = low[:, :LANES] + other_half(high_part[:, :LANES])
        odd_sum = low[:, LANES:] + other_half(high_part[:, LANES:])
        ahead = jnp.where(left, even_sum, other_half(odd_sum))
        behind = jnp.where(left, odd_sum, other_half(even_sum))
        tile = jnp.where(odd, behind, ahead)
        for mask in range(4):
            at = pl.ds(pl.multiple_of((own ^ mask) * high, high), high)
            total_ref[pair, at] = tile[high * mask : high * mask + high]
        to = pl.ds(pl.multiple_of(((own_row // 2) ^ pair) * LANES, LANES), LANES)
        done += fetch(((total_ref.at[pair], out_hbm.at[:, to]),), out_sems.at[pl.ds(pair, 1)])
    finish(done)


def call(
    kernel, outs, scalars, *arrays, small=(), small_outs=(), scratch=(), dmas=(8,)
):
    vmem = pl.BlockSpec(memory_space=pltpu.VMEM)
    smem = pl.BlockSpec(memory_space=pltpu.SMEM)
    hbm = pl.BlockSpec(memory_space=pltpu.HBM)
    return pl.pallas_call(
        kernel,
        out_shape=list(outs) + list(small_outs),
        in_specs=[smem] * len(scalars) + [hbm] * len(arrays) + [vmem] * len(small),
        out_specs=[hbm] * len(outs) + [vmem] * len(small_outs),
        scratch_shapes=[pltpu.VMEM(a.shape, a.dtype) for a in scratch]
        + [pltpu.SemaphoreType.DMA((count,)) for count in dmas],
        compiler_params=pltpu.CompilerParams(vmem_limit_bytes=LIMIT),
        cost_estimate=pl.CostEstimate(
            flops=1, bytes_accessed=1, transcendentals=0
        ),
        name=kernel.__name__.removesuffix("_kernel"),
    )(*scalars, *arrays, *small)


def shaped(shape, dtype):
    return jax.ShapeDtypeStruct(shape, dtype)


def gathered_pairs(block, axis):
    near = swap_bits(block, axis, 1)
    far = swap_bits(block, axis, 2)
    return [block, near, far, swap_bits(far, axis, 1)]


def on_device_packed(
    query_proj, key_proj, value_proj, short_filter, long_filter, skip_gain, out_weight, cotangent
):
    peers = lax.axis_size("seq")
    rows, channels = query_proj.shape
    features = cotangent.shape[1]
    size = peers * rows
    seq_at, ch_at = lax.axis_index("seq"), lax.axis_index("ch")
    ids = jnp.stack([seq_at, ch_at]).astype(jnp.int32)
    forward_table, inverse_table = (jnp.asarray(table) for table in wave_tables(size))
    cots = gathered_pairs(cotangent, "ch")

    own_short = lax.dynamic_slice_in_dim(short_filter, seq_at * HALF, HALF, 2)
    own_skip = lax.dynamic_slice_in_dim(skip_gain, seq_at * HALF, HALF, 0)[None]
    unit = (lax.broadcasted_iota(jnp.int32, (3, HALF), 0) == 0).astype(F32)
    wq, wk, wv = own_short[0], own_short[1], own_short[2]
    prm = jnp.concatenate(
        [
            jnp.concatenate([wk, wv, wk, wq, own_skip], axis=0),
            jnp.concatenate([wq, unit, wv, unit, own_skip], axis=0),
        ],
        axis=1,
    )

    inputs = (query_proj, key_proj, value_proj, long_filter)
    packs = shaped((peers, 2, rows, LANES), BF16)
    (packed,) = call(pack_streams_kernel, [packs], [], *inputs, scratch=(*inputs, packs))
    streams = lax.all_to_all(packed, "seq", 0, 0, tiled=True)
    weight_room = shaped((4, channels, features), BF16)
    sent = shaped((peers, rows // 2 + rows, LANES), BF16)
    (sent_grad,) = call(
        grad_gated_kernel,
        [sent],
        [ids],
        *cots,
        out_weight,
        small=(prm,),
        scratch=(*cots, weight_room, sent),
        dmas=(4, 4),
    )
    moved_grad = lax.all_to_all(sent_grad, "seq", 0, 0, tiled=True)
    other_weight = swap_bits(out_weight, "ch", 1)
    moved_grad, other_weight = lax.optimization_barrier((moved_grad, other_weight))
    wide = shaped((size, LANES), F32)
    spectra = shaped((4, size // 2, LANES), F32)
    folds = shaped((peers // 2, rows, LANES), BF16)
    tables = (forward_table, inverse_table)
    results = [folds, wide, wide, wide, spectra]
    gated, kqs, vhs, mq, spec = call(
        forward_kernel,
        results,
        [],
        streams,
        *tables,
        sent_grad,
        small=(prm,),
        scratch=(packs, *tables, *results, wide, wide),
        dmas=(3, 5),
    )
    blocks = {0: gated} | {mask: swap_bits(gated, "seq", mask) for mask in (4, 2, 1)}
    backs = shaped((peers, 2 * rows + 16, LANES), BF16)
    saved = (mq, spec, kqs, vhs, streams, *tables)
    (back,) = call(
        backward_kernel,
        [backs],
        [],
        moved_grad,
        *saved,
        small=(prm,),
        scratch=(
            shaped((peers, rows // 2, LANES), BF16), *saved, backs, wide, spectra, wide
        ),
    )
    back, blocks = lax.optimization_barrier((back, blocks))
    blocks[6] = swap_bits(blocks[4], "seq", 2)
    blocks[3], blocks[5] = swap_bits(blocks[2], "seq", 1), swap_bits(blocks[4], "seq", 1)
    cot_rows = moved_grad[:, rows // 2 :]
    blocks[6], cot_rows = lax.optimization_barrier((blocks[6], cot_rows))
    blocks[7] = swap_bits(blocks[6], "seq", 1)
    gates = [blocks[at] for at in range(8)]
    near, far = swap_bits(cot_rows, "ch", 1), swap_bits(cot_rows, "ch", 2)
    other_gates = [swap_bits(block, "ch", 1) for block in gates]
    back, gates, other_gates[:7] = lax.optimization_barrier((back, gates, other_gates[:7]))
    returned = lax.all_to_all(back, "seq", 0, 0, tiled=True)
    sums = [shaped((rows, features), F32), shaped((rows, features), BF16)]
    keep, away = call(
        project_kernel,
        sums,
        [ids],
        *gates,
        *other_gates,
        out_weight,
        other_weight,
        scratch=(
            shaped((2 * peers, rows, LANES), BF16),
            weight_room,
            *sums,
            shaped((2, rows, channels), BF16),
        ),
        dmas=(16, 4),
    )
    share = swap_bits(away, "ch", 2)
    far, near, away = lax.optimization_barrier((far, near, away))
    cot_parts = [cot_rows, near, far, swap_bits(far, "ch", 1)]
    plain = shaped((rows, channels), F32)
    grad_query, grad_key, grad_value, grad_filter, grad_short, grad_skip = call(
        unpack_kernel,
        [plain] * 4,
        [],
        returned,
        small_outs=[shaped((3, 3, channels), F32), shaped((1, channels), F32)],
        scratch=(backs, plain, plain, plain, plain),
    )
    (grad_w_out_t,) = call(
        grad_weight_kernel,
        [shaped((4 * LANES, channels), F32)],
        [ids],
        *cot_parts,
        *gates,
        scratch=(
            shaped((4, peers, LANES, rows), BF16),
            shaped((peers // 2, peers // 2, rows, 2 * LANES), BF16),
            shaped((2, 4 * LANES, peers // 2 * rows), BF16),
            shaped((peers // 2, 4 * LANES, LANES), F32),
        ),
        dmas=(12, 4),
    )
    share, grad_w_out_t, grad_filter = lax.optimization_barrier(
        (share, grad_w_out_t, grad_filter)
    )
    layer_out = (keep + share.astype(F32)).astype(BF16)
    return (
        layer_out,
        grad_query,
        grad_key,
        grad_value,
        grad_short,
        grad_filter,
        grad_skip[0],
        grad_w_out_t,
    )


def solution(mesh):
    in_specs = (
        P("seq", "ch"),
        P("seq", "ch"),
        P("seq", "ch"),
        P(None, None, "ch"),
        P("seq", "ch"),
        P("ch"),
        P("ch", None),
        P("seq", "ch"),
    )
    out_specs = (
        P("seq", "ch"),
        P("seq", "ch"),
        P("seq", "ch"),
        P("seq", "ch"),
        P(None, None, "ch"),
        P("seq", "ch"),
        P("ch"),
        P("seq", "ch"),
    )
    split = dict(mesh.shape)

    def whole(*arrays):
        rows = arrays[0].shape[0] // split["seq"]
        channels = arrays[0].shape[1] // split["ch"]
        features = arrays[7].shape[1]
        packs = (
            split["ch"] == 4
            and channels == HALF * split["seq"]
            and features == 4 * LANES * split["seq"]
            and arrays[0].shape[0] <= 1024
            and rows % 16 == 0
            and arrays[3].shape[1] == 3
        )
        body = on_device_packed if packs else on_device
        return jax.shard_map(
            body,
            mesh=mesh,
            in_specs=in_specs,
            out_specs=out_specs,
            check_vma=False,
        )(*arrays)

    return whole
```

```python
import functools
import math

import jax
import jax.numpy as jnp
import ml_dtypes
import numpy as np
from jax import lax
from jax.experimental import pallas as pl
from jax.experimental.pallas import tpu as pltpu
from jax.sharding import PartitionSpec as P

exact_mode = lax.Precision.HIGHEST


def from_behind(shard, axis, by):
    size = lax.axis_size(axis)
    pairs = [(i, i + by) for i in range(size) if 0 <= i + by < size]
    return lax.ppermute(shard, axis, pairs)


def as_sent(shard):

    def short(part):
        return part.astype(jnp.bfloat16) if part.dtype == jnp.float32 else part

    return jax.tree.map(short, shard)


def tables(rows_out, cols_in, period):
    row_index = lax.broadcasted_iota(jnp.int32, (rows_out, cols_in), 0)
    col_index = lax.broadcasted_iota(jnp.int32, (rows_out, cols_in), 1)
    phase_angle = (row_index * col_index % period).astype(jnp.float32) * (2.0 * math.pi / period)
    return (jnp.cos(phase_angle), jnp.sin(phase_angle))


def along_rows(factor, values):
    return jnp.tensordot(factor, values, axes=1, precision=exact_mode)


def rows_spectrum(signal, basis_pair):
    return (along_rows(basis_pair[0], signal), -along_rows(basis_pair[1], signal))


def rows_inverse(complex_pair, basis_pair):
    total = along_rows(basis_pair[0], complex_pair[0]) - along_rows(basis_pair[1], complex_pair[1])
    return total / basis_pair[0].shape[1]


def block_forward(complex_pair, basis_pair):
    cosine_part, sine_part = basis_pair
    real_part = along_rows(cosine_part, complex_pair[0]) + along_rows(sine_part, complex_pair[1])
    imag_part = along_rows(cosine_part, complex_pair[1]) - along_rows(sine_part, complex_pair[0])
    return (real_part, imag_part)


def block_inverse(complex_pair, basis_pair):
    cosine_part, sine_part = basis_pair
    norming = 1.0 / cosine_part.shape[1]
    real_part = along_rows(cosine_part, complex_pair[0]) - along_rows(sine_part, complex_pair[1])
    imag_part = along_rows(cosine_part, complex_pair[1]) + along_rows(sine_part, complex_pair[0])
    return (real_part * norming, imag_part * norming)


def complex_product(first_pair, second_pair):
    return (
        first_pair[0] * second_pair[0] - first_pair[1] * second_pair[1],
        first_pair[0] * second_pair[1] + first_pair[1] * second_pair[0],
    )


def conj_product(first_pair, second_pair):
    return (
        first_pair[0] * second_pair[0] + first_pair[1] * second_pair[1],
        first_pair[0] * second_pair[1] - first_pair[1] * second_pair[0],
    )


def on_device(
    query_proj, key_proj, value_proj, short_filter, long_filter, skip_gain, out_weight, cotangent
):
    block_rows = query_proj.shape[0]
    tap_count = short_filter.shape[1]
    block_count = lax.axis_size("seq")
    streams = jnp.stack([query_proj, key_proj, value_proj])
    earlier = from_behind(streams[:, block_rows - (tap_count - 1) :], "seq", 1)
    extended = jnp.concatenate([earlier, streams], axis=1).astype(jnp.float32)
    shifted = [
        extended[:, tap_count - 1 - offset : tap_count - 1 - offset + block_rows]
        for offset in range(tap_count)
    ]
    filtered = sum(
        (short_filter[:, offset][:, None, :] * shifted[offset] for offset in range(tap_count))
    )
    query_short, key_short, value_short = (filtered[0], filtered[1], filtered[2])
    product = key_short * value_short
    forward_basis = tables(2 * block_rows, block_rows, 2 * block_rows)
    full_basis = tables(2 * block_rows, 2 * block_rows, 2 * block_rows)
    half_basis = tables(block_rows, 2 * block_rows, 2 * block_rows)
    block_basis = tables(2 * block_count, block_count, 2 * block_count)
    return_basis = tables(block_count, 2 * block_count, 2 * block_count)
    input_pair = rows_spectrum(product, forward_basis)
    filter_pair = rows_spectrum(long_filter, forward_basis)
    moved_data = (
        lax.all_to_all(input_pair[0][None], "seq", split_axis=1, concat_axis=0, tiled=True),
        lax.all_to_all(input_pair[1][None], "seq", split_axis=1, concat_axis=0, tiled=True),
        lax.all_to_all(filter_pair[0][None], "seq", split_axis=1, concat_axis=0, tiled=True),
        lax.all_to_all(filter_pair[1][None], "seq", split_axis=1, concat_axis=0, tiled=True),
    )
    input_spectrum = block_forward((moved_data[0], moved_data[1]), block_basis)
    filter_spectrum = block_forward((moved_data[2], moved_data[3]), block_basis)
    inverse_pair = block_inverse(complex_product(filter_spectrum, input_spectrum), return_basis)
    returned = (
        lax.all_to_all(inverse_pair[0], "seq", split_axis=0, concat_axis=1, tiled=True),
        lax.all_to_all(inverse_pair[1], "seq", split_axis=0, concat_axis=1, tiled=True),
    )
    folded = rows_inverse((returned[0][0], returned[1][0]), full_basis)
    carried = from_behind(folded[block_rows:], "seq", 1)
    convolved = folded[:block_rows] + carried
    mixed_seq = convolved + skip_gain * product
    gated_values = (query_short * mixed_seq).astype(jnp.bfloat16)
    partial_value = jnp.dot(gated_values, out_weight, preferred_element_type=jnp.float32)
    layer_out = lax.psum_scatter(partial_value, "ch", scatter_dimension=1, tiled=True).astype(
        jnp.bfloat16
    )
    full_cotangent = lax.all_gather(cotangent, "ch", axis=1, tiled=True)
    grad_gated = lax.dot_general(
        full_cotangent, out_weight, (((1,), (1,)), ((), ())), preferred_element_type=jnp.float32
    )
    grad_w_out_t = lax.psum_scatter(
        lax.dot_general(
            full_cotangent,
            gated_values,
            (((0,), (0,)), ((), ())),
            preferred_element_type=jnp.float32,
        ),
        "seq",
        scatter_dimension=0,
        tiled=True,
    )
    grad_mixed = grad_gated * query_short
    grad_query_short = grad_gated * mixed_seq
    following = from_behind(grad_mixed.astype(jnp.bfloat16), "seq", -1).astype(grad_mixed.dtype)
    spread = jnp.concatenate([grad_mixed, following], axis=0)
    grad_pair = rows_spectrum(spread, full_basis)
    moved_grad = (
        lax.all_to_all(
            grad_pair[0][None].astype(jnp.bfloat16), "seq", split_axis=1, concat_axis=0, tiled=True
        ).astype(jnp.float32),
        lax.all_to_all(
            grad_pair[1][None].astype(jnp.bfloat16), "seq", split_axis=1, concat_axis=0, tiled=True
        ).astype(jnp.float32),
    )
    grad_spectrum = block_forward(moved_grad, block_basis)
    input_back = block_inverse(conj_product(filter_spectrum, grad_spectrum), return_basis)
    filter_back = block_inverse(conj_product(input_spectrum, grad_spectrum), return_basis)
    returned_grad = (
        lax.all_to_all(as_sent(input_back[0]), "seq", split_axis=0, concat_axis=1, tiled=True),
        lax.all_to_all(as_sent(input_back[1]), "seq", split_axis=0, concat_axis=1, tiled=True),
        lax.all_to_all(as_sent(filter_back[0]), "seq", split_axis=0, concat_axis=1, tiled=True),
        lax.all_to_all(as_sent(filter_back[1]), "seq", split_axis=0, concat_axis=1, tiled=True),
    )
    conv_grad = rows_inverse((returned_grad[0][0], returned_grad[1][0]), half_basis)
    grad_filter = rows_inverse((returned_grad[2][0], returned_grad[3][0]), half_basis)
    grad_product = conv_grad + skip_gain * grad_mixed
    grad_streams = jnp.stack(
        [grad_query_short, grad_product * value_short, grad_product * key_short]
    )
    later_rows = from_behind(grad_streams[:, : tap_count - 1], "seq", -1)
    padded_grad = jnp.concatenate([grad_streams, later_rows], axis=1)
    grad_inputs = sum(
        (
            short_filter[:, offset][:, None, :] * padded_grad[:, offset : offset + block_rows]
            for offset in range(tap_count)
        )
    )
    short_terms = jnp.stack(
        [jnp.sum(grad_streams * shifted[offset], axis=1) for offset in range(tap_count)], axis=1
    )
    skip_terms = jnp.sum(grad_mixed * product, axis=0)
    grad_short, grad_skip = lax.psum((short_terms, skip_terms), "seq")
    return (
        layer_out,
        grad_inputs[0],
        grad_inputs[1],
        grad_inputs[2],
        grad_short,
        grad_filter,
        grad_skip,
        grad_w_out_t,
    )


LANES = 128
HALF = 64
LIMIT = 63 * 2**20 + 2**19
F32 = jnp.float32
BF16 = jnp.bfloat16


def swap_bits(shard, axis, mask):
    size = lax.axis_size(axis)
    return lax.ppermute(shard, axis, [(i, i ^ mask) for i in range(size)])


@functools.lru_cache
def wave_tables(rows):
    half = rows // 2
    steps = np.outer(2 * np.arange(half) + 1, np.arange(rows)) % (4 * rows)
    angle = steps * (math.pi / (2 * rows))
    waves = np.concatenate([np.cos(angle), np.sin(angle)], axis=0)
    split = np.stack([waves[:, 0::2], waves[:, 1::2]])
    inverse = np.swapaxes(split, 1, 2) / rows
    return split.astype(ml_dtypes.bfloat16), inverse.astype(ml_dtypes.bfloat16)


def left_lanes(rows):
    return lax.broadcasted_iota(jnp.int32, (rows, LANES), 1) < HALF


def other_half(block):
    return pltpu.roll(block, HALF, 1)


def earlier_rows(block, by):
    if by == 0:
        return block
    row = lax.broadcasted_iota(jnp.int32, block.shape, 0)
    return jnp.where(row >= by, pltpu.roll(block, by, 0), 0.0)


def later_rows(block, by):
    if by == 0:
        return block
    size = block.shape[0]
    row = lax.broadcasted_iota(jnp.int32, block.shape, 0)
    return jnp.where(row < size - by, pltpu.roll(block, size - by, 0), 0.0)


def spectrum(table_ref, signal_ref, out_ref):
    half = table_ref.shape[2]
    quarter = 256
    even = signal_ref[pl.ds(0, half, stride=2)].astype(BF16)
    odd = signal_ref[pl.ds(1, half, stride=2)].astype(BF16)
    for start in range(0, 2 * half, quarter):
        at = slice(start, start + quarter)
        first = jnp.dot(table_ref[0, at], even, preferred_element_type=F32)
        second = jnp.dot(table_ref[1, at], odd, preferred_element_type=F32)
        kind, row = (0, start) if start < half else (2, start - half)
        out_ref[kind, row : row + quarter] = first + second
        mirrored = first - second if kind == 0 else second - first
        out_ref[kind + 1, row : row + quarter] = mirrored


def from_spectrum(table_ref, parts, out_ref):
    half = table_ref.shape[1]
    quarter = 256
    cosine, cosine_mirror, sine, sine_mirror = parts
    even = jnp.concatenate([cosine + cosine_mirror, sine - sine_mirror], axis=0).astype(BF16)
    odd = jnp.concatenate([cosine - cosine_mirror, sine + sine_mirror], axis=0).astype(BF16)
    for side, operand in enumerate((even, odd)):
        for start in range(0, half, quarter):
            out_ref[pl.ds(2 * start + side, quarter, stride=2)] = jnp.dot(
                table_ref[side, start : start + quarter], operand, preferred_element_type=F32
            )


def fetch(pairs, sems):
    copies = [
        pltpu.make_async_copy(source, target, sems.at[at])
        for at, (source, target) in enumerate(pairs)
    ]
    for copy in copies:
        copy.start()
    return copies


def finish(copies):
    for copy in copies:
        copy.wait()


def pack_streams_kernel(q_hbm, k_hbm, v_hbm, h_hbm, out_hbm, q_ref, k_ref, v_ref, h_ref, out_ref, sems):
    copies = fetch(((k_hbm, k_ref), (q_hbm, q_ref), (v_hbm, v_ref), (h_hbm, h_ref)), sems)
    rows = q_ref.shape[0]
    left = left_lanes(rows)
    for at, (first_ref, second_ref) in enumerate(((k_ref, q_ref), (v_ref, h_ref))):
        copies[2 * at].wait()
        copies[2 * at + 1].wait()
        for peer in range(out_ref.shape[0]):
            lanes = slice(LANES * (peer // 2), LANES * (peer // 2) + LANES)
            first = first_ref[:, lanes].astype(F32)
            second = second_ref[:, lanes].astype(F32)
            if peer % 2 == 0:
                both = jnp.where(left, first, other_half(second))
            else:
                both = jnp.where(left, other_half(first), second)
            out_ref[peer, at] = both.astype(BF16)
    finish(fetch(((out_ref, out_hbm),), sems))


def fold_rows(block):
    half = block.shape[0] // 2
    return jnp.where(left_lanes(half), block[:half], other_half(block[half:]))


def unfold_rows(folds):
    blocks, half, _ = folds.shape
    turned = pltpu.roll(folds, HALF, 2)
    left = lax.broadcasted_iota(jnp.int32, folds.shape, 2) < HALF
    both = [jnp.where(left, folds, turned), jnp.where(left, turned, folds)]
    return jnp.concatenate(both, axis=1).reshape(blocks * 2 * half, LANES)


def column_parts(w_hbm, w_ref, order, mine, sems):
    width = w_ref.shape[2]
    places = [pl.multiple_of((mine ^ mask) * width, width) for mask in order]
    return fetch(
        [(w_hbm.at[:, pl.ds(at, width)], w_ref.at[n]) for n, at in enumerate(places)], sems
    )


def grad_gated_kernel(
    c0_hbm, c1_hbm, c2_hbm, c3_hbm, w_hbm, send_hbm,
    c0_ref, c1_ref, c2_ref, c3_ref, w_ref, send_ref, cot_sems, sems,
):
    mine = lax.axis_index("ch")
    cots = (c0_ref, c1_ref, c2_ref, c3_ref)
    loads = fetch(zip((c0_hbm, c1_hbm, c2_hbm, c3_hbm), cots), cot_sems)
    copies = column_parts(w_hbm, w_ref, range(4), mine, sems)
    rows = c0_ref.shape[0]
    for mask, part_ref in enumerate(cots):
        loads[mask].wait()
        for half in range(2):
            at = pl.multiple_of(half * 4 * LANES + mine * LANES, LANES)
            turned = part_ref[:, pl.ds(at, LANES)].astype(F32).T
            send_ref[2 * (mine ^ mask) + half, rows // 2 :] = turned.astype(BF16)
    total = None
    for mask, part_ref in enumerate(cots):
        copies[mask].wait()
        term = lax.dot_general(
            part_ref[...], w_ref[mask], (((1,), (1,)), ((), ())), preferred_element_type=F32
        )
        total = term if total is None else total + term
    for peer in range(send_ref.shape[0]):
        tile = total[:, LANES * (peer // 2) : LANES * (peer // 2) + LANES]
        if peer % 2 == 1:
            tile = other_half(tile)
        send_ref[peer, : rows // 2] = fold_rows(tile).astype(BF16)
    finish(fetch(((send_ref, send_hbm),), sems))


def forward_kernel(
    moved_hbm, fwd_hbm, inv_hbm, after_hbm, prm_ref,
    send_hbm, kqs_hbm, vhs_hbm, mq_hbm, spec_hbm,
    moved_ref, fwd_ref, inv_ref, send_ref, kqs_ref, vhs_ref, mq_ref, spec_ref,
    signal_ref, y_ref, sems, out_sems,
):
    copies = fetch(((moved_hbm, moved_ref), (fwd_hbm, fwd_ref), (inv_hbm, inv_ref)), sems)
    peers, _, rows, _ = moved_ref.shape
    size = peers * rows
    left = left_lanes(size)
    copies[0].wait()
    kq = moved_ref[:, 0].reshape(size, LANES).astype(F32)
    vh = moved_ref[:, 1].reshape(size, LANES).astype(F32)
    kqs = sum(prm_ref[j : j + 1] * earlier_rows(kq, j) for j in range(3))
    vhs = sum(prm_ref[3 + j : 4 + j] * earlier_rows(vh, j) for j in range(3))
    kqs_ref[...] = kqs
    vhs_ref[...] = vhs
    done = fetch(((kqs_ref, kqs_hbm), (vhs_ref, vhs_hbm)), out_sems)
    product = kqs * vhs
    signal_ref[...] = jnp.where(left, product, vhs)
    copies[1].wait()
    spectrum(fwd_ref, signal_ref, spec_ref)
    done += fetch(((spec_ref, spec_hbm),), out_sems.at[pl.ds(2, 1)])
    parts = [None] * 4
    for mirror in range(2):
        xc, xs = spec_ref[mirror], spec_ref[2 + mirror]
        hc, hs = other_half(xc), other_half(xs)
        parts[mirror] = xc * hc - xs * hs
        parts[2 + mirror] = xc * hs + xs * hc
    copies[2].wait()
    from_spectrum(inv_ref, parts, y_ref)
    both_product = jnp.where(left, product, other_half(product))
    mixed = y_ref[...] + prm_ref[12:13] * both_product
    mq_ref[...] = jnp.where(left, mixed, kqs)
    gated = kqs * mixed
    left_rows = left_lanes(rows)
    for pair in range(peers // 2):
        first = gated[2 * rows * pair : 2 * rows * pair + rows]
        second = gated[2 * rows * pair + rows : 2 * rows * (pair + 1)]
        send_ref[pair] = jnp.where(left_rows, other_half(first), second).astype(BF16)
    done += fetch(((mq_ref, mq_hbm), (send_ref, send_hbm)), out_sems.at[pl.ds(3, 2)])
    finish(done)


def project_kernel(ids_ref, *refs):
    gates = refs[:16]
    w_hbm, other_hbm, keep_hbm, away_hbm = refs[16:20]
    gate_ref, w_ref, keep_ref, away_ref, gated_ref, gate_sems, sems = refs[20:]
    own_row, mine = ids_ref[0], ids_ref[1]
    loads = fetch(
        [(gate.at[own_row // 2], gate_ref.at[at]) for at, gate in enumerate(gates)], gate_sems
    )
    width = keep_ref.shape[1]
    copies = []
    for n, (hbm, mask) in enumerate(((w_hbm, 2), (other_hbm, 2), (w_hbm, 0), (other_hbm, 0))):
        at = pl.multiple_of((mine ^ mask) * width, width)
        copies += fetch(((hbm.at[:, pl.ds(at, width)], w_ref.at[n]),), sems.at[pl.ds(n, 1)])
    left = left_lanes(gate_ref.shape[1])
    odd = own_row % 2 == 1
    for side in range(2):
        finish(loads[8 * side : 8 * side + 8])
        for pair in range(4):
            one = gate_ref[8 * side + 2 * pair].astype(F32)
            two = gate_ref[8 * side + 2 * pair + 1].astype(F32)
            even_rows = jnp.where(left, one, other_half(two))
            odd_rows = jnp.where(left, other_half(two), one)
            lanes = pl.ds(pl.multiple_of(((own_row // 2) ^ pair) * LANES, LANES), LANES)
            gated_ref[side, :, lanes] = jnp.where(odd, odd_rows, even_rows).astype(BF16)
    done = []
    for n, (out_ref, out_hbm) in enumerate(((away_ref, away_hbm), (keep_ref, keep_hbm))):
        total = None
        for side in range(2):
            copies[2 * n + side].wait()
            part = jnp.dot(gated_ref[side], w_ref[2 * n + side], preferred_element_type=F32)
            total = part if total is None else total + part
        out_ref[...] = total.astype(out_ref.dtype)
        done += fetch(((out_ref, out_hbm),), gate_sems.at[pl.ds(n, 1)])
    finish(done)


def backward_kernel(
    moved_hbm, mq_hbm, spec_hbm, kqs_hbm, vhs_hbm, streams_hbm, fwd_hbm, inv_hbm, prm_ref,
    send_hbm,
    moved_ref, mq_ref, spec_ref, kqs_ref, vhs_ref, streams_ref, fwd_ref, inv_ref, send_ref,
    signal_ref, mspec_ref, back_ref, sems,
):
    copies = fetch(
        (
            (moved_hbm.at[:, pl.ds(0, moved_ref.shape[1])], moved_ref),
            (mq_hbm, mq_ref),
            (fwd_hbm, fwd_ref),
            (spec_hbm, spec_ref),
            (inv_hbm, inv_ref),
            (kqs_hbm, kqs_ref),
            (vhs_hbm, vhs_ref),
            (streams_hbm, streams_ref),
        ),
        sems,
    )
    peers, _, rows, _ = streams_ref.shape
    size = peers * rows
    left = left_lanes(size)
    finish(copies[:2])
    z = unfold_rows(moved_ref[...].astype(F32)) * mq_ref[...]
    grad_mixed = jnp.where(left, other_half(z), z)
    signal_ref[...] = grad_mixed
    copies[2].wait()
    spectrum(fwd_ref, signal_ref, mspec_ref)
    copies[3].wait()
    parts = [None] * 4
    for mirror in range(2):
        xc, xs = spec_ref[mirror], spec_ref[2 + mirror]
        mc, ms = mspec_ref[mirror], mspec_ref[2 + mirror]
        parts[mirror] = xc * mc + xs * ms
        parts[2 + mirror] = xc * ms - xs * mc
    copies[4].wait()
    from_spectrum(inv_ref, parts, back_ref)
    finish(copies[5:])
    back = back_ref[...]
    kqs, vhs = kqs_ref[...], vhs_ref[...]
    grad_product = back + prm_ref[12:13] * grad_mixed
    grad_product = jnp.where(left, other_half(grad_product), grad_product)
    grad_kv = grad_product * jnp.where(left, vhs, other_half(kqs))
    grad_qf = jnp.where(left, z, other_half(back))
    kq = streams_ref[:, 0].reshape(size, LANES).astype(F32)
    vh = streams_ref[:, 1].reshape(size, LANES).astype(F32)
    raw_kv = jnp.where(left, kq, other_half(vh))
    raw_q = other_half(kq)
    out_kv = sum(prm_ref[6 + j : 7 + j] * later_rows(grad_kv, j) for j in range(3))
    out_qf = sum(prm_ref[9 + j : 10 + j] * later_rows(grad_qf, j) for j in range(3))
    sums = [jnp.sum(grad_kv * earlier_rows(raw_kv, j), axis=0, keepdims=True) for j in range(3)]
    sums += [jnp.sum(grad_qf * earlier_rows(raw_q, j), axis=0, keepdims=True) for j in range(3)]
    sums += [jnp.sum(grad_mixed * kqs * vhs, axis=0, keepdims=True)]
    sums += [jnp.zeros_like(sums[0])]
    small = jnp.concatenate(sums, axis=0)
    small_high = small.astype(BF16).astype(F32)
    small = jnp.concatenate([small_high, small - small_high], axis=0).astype(BF16)
    for peer in range(peers):
        at = slice(rows * peer, rows * peer + rows)
        send_ref[peer, :rows] = out_kv[at].astype(BF16)
        send_ref[peer, rows : 2 * rows] = out_qf[at].astype(BF16)
        send_ref[peer, 2 * rows :] = small
    finish(fetch(((send_ref, send_hbm),), sems))


def unpack_kernel(
    moved_hbm, q_hbm, k_hbm, v_hbm, f_hbm, short_ref, skip_ref,
    moved_ref, q_ref, k_ref, v_ref, f_ref, sems,
):
    finish(fetch(((moved_hbm, moved_ref),), sems))
    peers = moved_ref.shape[0]
    rows = q_ref.shape[0]
    left = left_lanes(rows)
    left_few = left_lanes(8)

    def merged(first, second, mask):
        return (
            jnp.where(mask, first, other_half(second)),
            jnp.where(mask, other_half(first), second),
        )

    tiles = range(peers // 2)
    for tile in tiles:
        lanes = slice(LANES * tile, LANES * tile + LANES)
        first, second = (moved_ref[2 * tile + n, :rows].astype(F32) for n in range(2))
        k_ref[:, lanes], v_ref[:, lanes] = merged(first, second, left)
    done = fetch(((k_ref, k_hbm), (v_ref, v_hbm)), sems)
    for tile in tiles:
        lanes = slice(LANES * tile, LANES * tile + LANES)
        first, second = (moved_ref[2 * tile + n, rows : 2 * rows].astype(F32) for n in range(2))
        q_ref[:, lanes], f_ref[:, lanes] = merged(first, second, left)
        few = [moved_ref[2 * tile + n, 2 * rows :].astype(F32) for n in range(2)]
        low, high = merged(few[0][:8] + few[0][8:], few[1][:8] + few[1][8:], left_few)
        short_ref[0, :, lanes] = low[3:6]
        short_ref[1, :, lanes] = low[0:3]
        short_ref[2, :, lanes] = high[0:3]
        skip_ref[:, lanes] = low[6:7]
    done += fetch(((q_ref, q_hbm), (f_ref, f_hbm)), sems.at[pl.ds(2, 2)])
    finish(done)


def grad_weight_kernel(ids_ref, *refs):
    cots, gates = refs[:4], refs[4:12]
    out_hbm, cot_ref, gate_ref, side_ref, total_ref, sems, out_sems = refs[12:]
    own_row, own = ids_ref[0], ids_ref[1]
    lanes = [pl.ds(LANES * half, LANES) for half in range(2)]
    copies = fetch(
        [(cot, cot_ref.at[at]) for at, cot in enumerate(cots)]
        + [
            (gate, gate_ref.at[at // 2, :, :, lanes[at % 2]]) for at, gate in enumerate(gates)
        ],
        sems,
    )
    _, peers, high, wide = cot_ref.shape
    left = left_lanes(4 * high)
    odd = own_row % 2 == 1
    for mask in range(4):
        copies[mask].wait()
        for peer in range(peers):
            at = slice(wide * (peer // 2), wide * (peer // 2) + wide)
            side_ref[peer % 2, high * mask : high * mask + high, at] = cot_ref[mask, peer]
    done = []
    for pair in range(peers // 2):
        finish(copies[4 + 2 * pair : 6 + 2 * pair])
        gate = gate_ref[pair].reshape(peers // 2 * wide, 2 * LANES)
        low = jnp.dot(side_ref[0], gate, preferred_element_type=F32)
        high_part = jnp.dot(side_ref[1], gate, preferred_element_type=F32)
        even_sum = low[:, :LANES] + other_half(high_part[:, :LANES])
        odd_sum = low[:, LANES:] + other_half(high_part[:, LANES:])
        ahead = jnp.where(left, even_sum, other_half(odd_sum))
        behind = jnp.where(left, odd_sum, other_half(even_sum))
        tile = jnp.where(odd, behind, ahead)
        for mask in range(4):
            at = pl.ds(pl.multiple_of((own ^ mask) * high, high), high)
            total_ref[pair, at] = tile[high * mask : high * mask + high]
        to = pl.ds(pl.multiple_of(((own_row // 2) ^ pair) * LANES, LANES), LANES)
        done += fetch(((total_ref.at[pair], out_hbm.at[:, to]),), out_sems.at[pl.ds(pair, 1)])
    finish(done)


def call(
    kernel, outs, scalars, *arrays, small=(), small_outs=(), scratch=(), dmas=(8,)
):
    vmem = pl.BlockSpec(memory_space=pltpu.VMEM)
    smem = pl.BlockSpec(memory_space=pltpu.SMEM)
    hbm = pl.BlockSpec(memory_space=pltpu.HBM)
    return pl.pallas_call(
        kernel,
        out_shape=list(outs) + list(small_outs),
        in_specs=[smem] * len(scalars) + [hbm] * len(arrays) + [vmem] * len(small),
        out_specs=[hbm] * len(outs) + [vmem] * len(small_outs),
        scratch_shapes=[pltpu.VMEM(a.shape, a.dtype) for a in scratch]
        + [pltpu.SemaphoreType.DMA((count,)) for count in dmas],
        compiler_params=pltpu.CompilerParams(vmem_limit_bytes=LIMIT),
        cost_estimate=pl.CostEstimate(
            flops=1, bytes_accessed=1, transcendentals=0
        ),
        name=kernel.__name__.removesuffix("_kernel"),
    )(*scalars, *arrays, *small)


def shaped(shape, dtype):
    return jax.ShapeDtypeStruct(shape, dtype)


def gathered_pairs(block, axis):
    near = swap_bits(block, axis, 1)
    far = swap_bits(block, axis, 2)
    return [block, near, far, swap_bits(far, axis, 1)]


def on_device_packed(
    query_proj, key_proj, value_proj, short_filter, long_filter, skip_gain, out_weight, cotangent
):
    peers = lax.axis_size("seq")
    rows, channels = query_proj.shape
    features = cotangent.shape[1]
    size = peers * rows
    seq_at, ch_at = lax.axis_index("seq"), lax.axis_index("ch")
    ids = jnp.stack([seq_at, ch_at]).astype(jnp.int32)
    forward_table, inverse_table = (jnp.asarray(table) for table in wave_tables(size))
    cots = gathered_pairs(cotangent, "ch")

    own_short = lax.dynamic_slice_in_dim(short_filter, seq_at * HALF, HALF, 2)
    own_skip = lax.dynamic_slice_in_dim(skip_gain, seq_at * HALF, HALF, 0)[None]
    unit = (lax.broadcasted_iota(jnp.int32, (3, HALF), 0) == 0).astype(F32)
    wq, wk, wv = own_short[0], own_short[1], own_short[2]
    prm = jnp.concatenate(
        [
            jnp.concatenate([wk, wv, wk, wq, own_skip], axis=0),
            jnp.concatenate([wq, unit, wv, unit, own_skip], axis=0),
        ],
        axis=1,
    )

    inputs = (query_proj, key_proj, value_proj, long_filter)
    packs = shaped((peers, 2, rows, LANES), BF16)
    (packed,) = call(pack_streams_kernel, [packs], [], *inputs, scratch=(*inputs, packs))
    streams = lax.all_to_all(packed, "seq", 0, 0, tiled=True)
    weight_room = shaped((4, channels, features), BF16)
    sent = shaped((peers, rows // 2 + rows, LANES), BF16)
    (sent_grad,) = call(
        grad_gated_kernel,
        [sent],
        [],
        *cots,
        out_weight,
        scratch=(*cots, weight_room, sent),
        dmas=(4, 4),
    )
    moved_grad = lax.all_to_all(sent_grad, "seq", 0, 0, tiled=True)
    other_weight = swap_bits(out_weight, "ch", 1)
    moved_grad, other_weight = lax.optimization_barrier((moved_grad, other_weight))
    wide = shaped((size, LANES), F32)
    spectra = shaped((4, size // 2, LANES), F32)
    folds = shaped((peers // 2, rows, LANES), BF16)
    tables = (forward_table, inverse_table)
    results = [folds, wide, wide, wide, spectra]
    gated, kqs, vhs, mq, spec = call(
        forward_kernel,
        results,
        [],
        streams,
        *tables,
        sent_grad,
        small=(prm,),
        scratch=(packs, *tables, *results, wide, wide),
        dmas=(3, 5),
    )
    blocks = {0: gated} | {mask: swap_bits(gated, "seq", mask) for mask in (4, 2, 1)}
    backs = shaped((peers, 2 * rows + 16, LANES), BF16)
    saved = (mq, spec, kqs, vhs, streams, *tables)
    (back,) = call(
        backward_kernel,
        [backs],
        [],
        moved_grad,
        *saved,
        small=(prm,),
        scratch=(
            shaped((peers, rows // 2, LANES), BF16), *saved, backs, wide, spectra, wide
        ),
    )
    back, blocks = lax.optimization_barrier((back, blocks))
    blocks[6] = swap_bits(blocks[4], "seq", 2)
    blocks[3], blocks[5] = swap_bits(blocks[2], "seq", 1), swap_bits(blocks[4], "seq", 1)
    cot_rows = moved_grad[:, rows // 2 :]
    blocks[6], cot_rows = lax.optimization_barrier((blocks[6], cot_rows))
    blocks[7] = swap_bits(blocks[6], "seq", 1)
    gates = [blocks[at] for at in range(8)]
    near, far = swap_bits(cot_rows, "ch", 1), swap_bits(cot_rows, "ch", 2)
    other_gates = [swap_bits(block, "ch", 1) for block in gates]
    back, gates, other_gates[:7] = lax.optimization_barrier((back, gates, other_gates[:7]))
    returned = lax.all_to_all(back, "seq", 0, 0, tiled=True)
    sums = [shaped((rows, features), F32), shaped((rows, features), BF16)]
    keep, away = call(
        project_kernel,
        sums,
        [ids],
        *gates,
        *other_gates,
        out_weight,
        other_weight,
        scratch=(
            shaped((2 * peers, rows, LANES), BF16),
            weight_room,
            *sums,
            shaped((2, rows, channels), BF16),
        ),
        dmas=(16, 4),
    )
    share = swap_bits(away, "ch", 2)
    far, near, away = lax.optimization_barrier((far, near, away))
    cot_parts = [cot_rows, near, far, swap_bits(far, "ch", 1)]
    plain = shaped((rows, channels), F32)
    grad_query, grad_key, grad_value, grad_filter, grad_short, grad_skip = call(
        unpack_kernel,
        [plain] * 4,
        [],
        returned,
        small_outs=[shaped((3, 3, channels), F32), shaped((1, channels), F32)],
        scratch=(backs, plain, plain, plain, plain),
    )
    (grad_w_out_t,) = call(
        grad_weight_kernel,
        [shaped((4 * LANES, channels), F32)],
        [ids],
        *cot_parts,
        *gates,
        scratch=(
            shaped((4, peers, LANES, rows), BF16),
            shaped((peers // 2, peers // 2, rows, 2 * LANES), BF16),
            shaped((2, 4 * LANES, peers // 2 * rows), BF16),
            shaped((peers // 2, 4 * LANES, LANES), F32),
        ),
        dmas=(12, 4),
    )
    share, grad_w_out_t, grad_filter = lax.optimization_barrier(
        (share, grad_w_out_t, grad_filter)
    )
    layer_out = (keep + share.astype(F32)).astype(BF16)
    return (
        layer_out,
        grad_query,
        grad_key,
        grad_value,
        grad_short,
        grad_filter,
        grad_skip[0],
        grad_w_out_t,
    )


def solution(mesh):
    in_specs = (
        P("seq", "ch"),
        P("seq", "ch"),
        P("seq", "ch"),
        P(None, None, "ch"),
        P("seq", "ch"),
        P("ch"),
        P("ch", None),
        P("seq", "ch"),
    )
    out_specs = (
        P("seq", "ch"),
        P("seq", "ch"),
        P("seq", "ch"),
        P("seq", "ch"),
        P(None, None, "ch"),
        P("seq", "ch"),
        P("ch"),
        P("seq", "ch"),
    )
    split = dict(mesh.shape)

    def whole(*arrays):
        rows = arrays[0].shape[0] // split["seq"]
        channels = arrays[0].shape[1] // split["ch"]
        features = arrays[7].shape[1]
        packs = (
            split["ch"] == 4
            and channels == HALF * split["seq"]
            and features == 4 * LANES * split["seq"]
            and arrays[0].shape[0] <= 1024
            and rows % 16 == 0
            and arrays[3].shape[1] == 3
        )
        body = on_device_packed if packs else on_device
        return jax.shard_map(
            body,
            mesh=mesh,
            in_specs=in_specs,
            out_specs=out_specs,
            check_vma=False,
        )(*arrays)

    return whole
```
